256 devices in a mesh: tile: 32 (over y, x, core), lev: 8 (over z).
Axes of the slice: x: 4, y: 4, z: 8, core: 2. Of those that a mesh axis runs over, the one named last changes fastest.
Arguments:
- conc: float32 [3, 48, 1024, 384], P(None, 'lev', 'tile'), may hold values from -6 to 6
- u_wind: float32 [48, 1024, 384], P('lev', 'tile'), may hold values from -0.15 to 0.15
- v_wind: float32 [48, 1024, 384], P('lev', 'tile'), may hold values from -0.15 to 0.15
- mixing: float32 [48, 1024, 384], P('lev', 'tile'), may hold values from 0.02 to 0.2
- kernels: float32 [8, 48], P(None, 'lev'), may hold values from 0.02 to 0.3
- observed: float32 [3, 32768], P(None, 'tile'), may hold values from -6 to 6
- obs_weight: float32 [32768], P('tile'), may hold values from 1 to 16
- column_tile: int32 [32768, 1], P('tile'), may hold values from 0 to 31; in each aligned block of 1024 rows (0 to 1023, 1024 to 2047, ...) at most 64 rows name the same one
- footprint: int32 [32768, 4], P('tile'), may hold values from 0 to 12287
- kernel_index: int32 [32768], P('tile'), may hold values from 0 to 7
Outputs:
- residual: float32 [3, 32768], P(None, 'tile')
- gradient: float32 [3, 48, 1024, 384], P(None, 'lev', 'tile')
The draws below stay inside these ranges and needn't reach their ends.
Inputs may be any that keep to these rules, and one draw needn't show every extreme that they name: `column_tile`: among the 1024 soundings of one tile, no column tile is named more than 64 times, and some column tile is named exactly 64 times. A footprint column is a longitude offset times 384 plus a latitude within the column tile.
All inputs are finite; a program needn't handle non-finite values.
Results may differ from the reference program's by a relative error of at most 0.00014.
Values sent between devices are 32-bit elements; how exact they have to be, the bound alone decides.
A program may use at most 192 MiB of HBM per device.

```python
import math
import jax
import jax.numpy as jnp
import numpy as np
from jax import lax

TRACERS = 3
LON_DEV = 32
NLAT = 384
SND_DEV = 1024
FOOT = 4
KERNELS = 8
LEVELS = 48
NLON = 1024
COLS_DEV = 12288
SOUNDINGS = 32768
CAP = 64
N_TILE = 32


def place_ends(entries, key, low, high):
    shape = entries.shape
    spot = [jax.random.randint(jax.random.fold_in(key, axis), (), 0, shape[axis]) for axis in range(len(shape))]
    entries = entries.at[tuple(spot)].set(low)
    longest = shape.index(max(shape))
    spot[longest] = (spot[longest] + 1) % shape[longest]
    return entries.at[tuple(spot)].set(high)


def shard_levels(key, shape, split, smallest, high):
    loudness, own = 1.0, jax.random.fold_in(key, 6)
    for dim, parts in split:
        draws = jnp.exp(jax.random.uniform(jax.random.fold_in(own, dim), (parts,), jnp.float32, smallest / len(split), high / len(split)))
        loudness = loudness * jnp.repeat(draws, shape[dim] // parts).reshape([-1 if axis == dim else 1 for axis in range(len(shape))])
    return loudness


def deal_out(key, own, number, rows, number_of, top, bound, skew):
    order = jax.random.permutation(key, number_of)
    heavy_load, ordinary = load_shares(number_of, rows * top, bound, skew, True), load_shares(number_of, rows * top, bound, skew, False)
    places = jnp.arange(number_of)

    def named(tallies, offset_by):
        used = int((tallies > 0).sum())
        fixed = max(1, used // 4)
        moved = fixed + (places - fixed + offset_by * (used - fixed)) % max(1, number_of - fixed)
        return jnp.zeros((number_of,), jnp.int32).at[order[jnp.where(places < fixed, places, moved)]].set(jnp.asarray(tallies, jnp.int32))

    tallies = jnp.where(number % 4 == 0, named(heavy_load, number // 4), named(ordinary, number - number // 4 - 1))
    mixed = jax.random.permutation(jax.random.fold_in(own, 3), number_of)
    donor, sink = mixed[0:number_of // 2 * 2:2], mixed[1:number_of // 2 * 2:2]
    margin = jnp.minimum(tallies[donor] - 1, bound - tallies[sink]) // 2
    margin = jnp.where((donor == order[0]) | (sink == order[0]) | (tallies[sink] == 0), 0, jnp.maximum(margin, 0))
    moved = jax.random.randint(jax.random.fold_in(own, 4), (number_of // 2,), 0, 1 << 20) % (margin + 1)
    tallies = tallies.at[donor].add(-moved).at[sink].add(moved)
    labels = jnp.searchsorted(jnp.cumsum(tallies), jnp.arange(rows * top), side="right").astype(jnp.int32)
    table = labels.reshape(top, rows).T
    table = table[jax.random.permutation(jax.random.fold_in(own, 1), rows)]
    offset_by = jax.random.randint(jax.random.fold_in(own, 2), (rows, 1), 0, top)
    return jnp.take_along_axis(table, (jnp.arange(top)[None, :] + offset_by) % top, axis=1)


def load_shares(count, total, bound, lean, full):
    weights = [(1 << 20) // math.isqrt(grade ** lean) + 1 for grade in range(1, count + 1)]
    largest = bound if full else min(bound, max(-(-total // count), total * weights[0] // sum(weights)))
    least = 1 if total - largest >= count - 1 else 0
    holding, surplus = [largest] + [least] * (count - 1), total - largest - least * (count - 1)
    while surplus > 0:
        free = [i for i in range(1, count) if holding[i] < largest] or [i for i in range(1, count) if holding[i] < bound]
        mass, remaining = sum([weights[i] for i in free]), surplus
        for i in free:
            extra = min(bound - holding[i], max(1, remaining * weights[i] // mass), surplus)
            holding[i] = holding[i] + extra
            surplus = surplus - extra
    return np.array(holding)


def centred(own_key, shape, spread, most, cuts=(), held_as=jnp.bfloat16):
    entries = jax.random.normal(own_key, shape, jnp.float32) * spread
    if len(cuts) > 0:
        entries = shard_levels(own_key, shape, cuts, -0.22, 0.18) * entries
    return jnp.clip(entries, min=-most, max=most).astype(held_as)


def setup_inputs(seed: int = 0) -> dict:
    splits = jax.random.split(jax.random.key(seed), 11)
    conc = centred(splits[0], (TRACERS, LEVELS, NLON, NLAT), 1.0, 6.0, ((1, 8), (2, 32)), jnp.float32)
    u_wind = jnp.clip(jax.random.uniform(splits[1], (LEVELS, NLON, NLAT), jnp.float32, -0.15, 0.15) * shard_levels(splits[1], (LEVELS, NLON, NLAT), ((0, 8), (1, 32)), -0.4, 0.0), -0.15, 0.15)
    v_wind = jnp.clip(jax.random.uniform(splits[2], (LEVELS, NLON, NLAT), jnp.float32, -0.15, 0.15) * shard_levels(splits[2], (LEVELS, NLON, NLAT), ((0, 8), (1, 32)), -0.4, 0.0), -0.15, 0.15)
    mixing = jnp.clip(jnp.exp(math.log(0.2) - 2.3025851 * jax.random.uniform(splits[3], (LEVELS, NLON, NLAT), jnp.float32) ** shard_levels(splits[3], (LEVELS, NLON, NLAT), ((0, 8), (1, 32)), -0.2, 0.2)), 0.02, 0.2)
    kernels = jnp.clip(jnp.exp(math.log(0.3) - 2.7080503 * jax.random.uniform(splits[4], (KERNELS, LEVELS), jnp.float32) ** shard_levels(splits[4], (KERNELS, LEVELS), ((1, 8),), -0.2, 0.2)), 0.02, 0.3)
    observed = centred(splits[5], (TRACERS, SOUNDINGS), 1.0, 6.0, ((1, 32),), jnp.float32)
    obs_weight = jnp.clip(jnp.exp(math.log(16.0) - 2.7725887 * jax.random.uniform(splits[6], (SOUNDINGS,), jnp.float32) ** shard_levels(splits[6], (SOUNDINGS,), ((0, 32),), -0.2, 0.2)), 1.0, 16.0)
    column_tile_keys = jax.random.split(jax.random.fold_in(splits[7], 1), SOUNDINGS // SND_DEV)
    column_tile_turns = jax.random.permutation(jax.random.fold_in(splits[7], 3), SOUNDINGS // SND_DEV)
    column_tile = jax.vmap(lambda own, number: deal_out(jax.random.fold_in(splits[7], 2), own, number, SND_DEV, N_TILE, 1, CAP, 1))(column_tile_keys, column_tile_turns).reshape((SOUNDINGS, 1))
    footprint = place_ends(jax.random.randint(splits[8], (SOUNDINGS, FOOT), 0, COLS_DEV), jax.random.fold_in(splits[8], 1), 0, COLS_DEV - 1).astype(jnp.int32)
    kernel_index = place_ends(jax.random.randint(splits[9], (SOUNDINGS,), 0, KERNELS), jax.random.fold_in(splits[9], 1), 0, KERNELS - 1).astype(jnp.int32)
    return {"conc": conc, "u_wind": u_wind, "v_wind": v_wind, "mixing": mixing, "kernels": kernels, "observed": observed, "obs_weight": obs_weight, "column_tile": column_tile, "footprint": footprint, "kernel_index": kernel_index}


def shift_north(values):
    return jnp.concatenate([values[..., 1:], jnp.zeros_like(values[..., :1])], -1)


def shift_south(values):
    return jnp.concatenate([jnp.zeros_like(values[..., :1]), values[..., :-1]], -1)


def face_parts(tracer_field, u_face, v_face, k_face):
    centre = tracer_field[..., 1:-1, 1:-1, :]
    east_cell = tracer_field[..., 1:-1, 2:, :]
    west_cell = tracer_field[..., 1:-1, :-2, :]
    upper_cell = tracer_field[..., 2:, 1:-1, :]
    lower_cell = tracer_field[..., :-2, 1:-1, :]
    open_face = (jnp.arange(tracer_field.shape[-1]) < tracer_field.shape[-1] - 1).astype(tracer_field.dtype)
    u_centre = u_face[1:-1, 1:-1, :]
    u_west = u_face[1:-1, :-2, :]
    v_centre = v_face[1:-1, 1:-1, :] * open_face
    k_centre = k_face[1:-1, 1:-1, :]
    k_lower = k_face[:-2, 1:-1, :]
    vertical = k_centre * (upper_cell - centre) - k_lower * (centre - lower_cell)
    return centre, east_cell, west_cell, u_centre, u_west, v_centre, vertical


def advance(tracer_field, u_face, v_face, k_face):
    centre, east_cell, west_cell, u_centre, u_west, v_centre, vertical = face_parts(tracer_field, u_face, v_face, k_face)
    flux_east = jnp.maximum(u_centre, 0.0) * centre + jnp.minimum(u_centre, 0.0) * east_cell
    flux_west = jnp.maximum(u_west, 0.0) * west_cell + jnp.minimum(u_west, 0.0) * centre
    flux_north = jnp.maximum(v_centre, 0.0) * centre + jnp.minimum(v_centre, 0.0) * shift_north(centre)
    return centre - flux_east + flux_west - flux_north + shift_south(flux_north) + vertical


def adjoint(tracer_field, u_face, v_face, k_face):
    centre, east_cell, west_cell, u_centre, u_west, v_centre, vertical = face_parts(tracer_field, u_face, v_face, k_face)
    along_lon = jnp.maximum(u_centre, 0.0) * (east_cell - centre) + jnp.minimum(u_west, 0.0) * (centre - west_cell)
    along_lat = jnp.maximum(v_centre, 0.0) * (shift_north(centre) - centre) + shift_south(jnp.minimum(v_centre, 0.0)) * (centre - shift_south(centre))
    return centre + along_lon + along_lat + vertical


def pad_cells(values):
    return jnp.pad(values, ((1, 1), (1, 1), (0, 0)))


def reference(conc, u_wind, v_wind, mixing, kernels, observed, obs_weight, column_tile, footprint, kernel_index):
    u_pad = pad_cells(u_wind)
    v_pad = pad_cells(v_wind)
    k_pad = pad_cells(mixing)

    def forward_one(tracer_field):
        halfway = advance(pad_cells(tracer_field), u_pad, v_pad, k_pad)
        return advance(pad_cells(halfway), u_pad, v_pad, k_pad)

    def adjoint_one(tracer_field):
        halfway = adjoint(pad_cells(tracer_field), u_pad, v_pad, k_pad)
        return adjoint(pad_cells(halfway), u_pad, v_pad, k_pad)

    evolved = lax.map(forward_one, conc)
    lon_index = column_tile[:, 0][:, None] * LON_DEV + footprint // NLAT
    flat_cells = (lon_index * NLAT + footprint % NLAT).astype(jnp.int32)
    all_columns = evolved.reshape(TRACERS, LEVELS, NLON * NLAT)
    picked = all_columns[:, :, flat_cells]
    profile = kernels[kernel_index].T
    model = jnp.einsum('tlsf,ls->ts', picked, profile, precision=lax.Precision.HIGHEST) / FOOT
    residual = model - observed
    weighted = obs_weight[None, :] * residual / FOOT
    flat_index = (kernel_index[:, None] * (NLON * NLAT) + flat_cells).astype(jnp.int32)
    term_rows = jnp.repeat(weighted[:, :, None], FOOT, axis=2).reshape(TRACERS, -1)
    summed = jnp.zeros((TRACERS, KERNELS * NLON * NLAT), jnp.float32).at[:, flat_index.reshape(-1)].add(term_rows)
    forcing = jnp.einsum('kl,tkc->tlc', kernels, summed.reshape(TRACERS, KERNELS, NLON * NLAT), precision=lax.Precision.HIGHEST)
    forcing = forcing.reshape(TRACERS, LEVELS, NLON, NLAT)
    gradient = lax.map(adjoint_one, forcing)
    return (residual, gradient)
```

```python
import functools

import jax
import jax.numpy as jnp
from jax import lax
from jax.experimental import pallas as pl
from jax.experimental.pallas import tpu as pltpu
from jax.sharding import PartitionSpec as P

MESH = pl.DeviceIdType.MESH
F32, BF16 = jnp.float32, jnp.bfloat16
NT = (((1,), (1,)), ((), ()))
TR, LV, LON, LAT = 3, 6, 32, 384
ROWS = TR * LV * LON
NTILE, NLEV, CAP, SND, FOOT = 32, 8, 64, 1024, 4
SLOTS = NTILE * CAP
CHUNK = SLOTS // NLEV
LOOK = FOOT * CHUNK


def parts_of(x, count):
    pieces = []
    for _ in range(count):
        piece = x.astype(BF16)
        pieces.append(piece)
        x = x - piece.astype(F32)
    return pieces


def kernel(
    conc, u_in, v_in, k_in, kern, fields,
    residual, gradient,
    x0, x1, x2, x3, u, v, k, lon_out, lon_in,
    ids_out, ids_in, hot, fa, fb, kw, lathot, lonhot, spread,
    e, picked, part_out, part_in, res, ret_in, terms, total,
    local_sem, halo_ss, halo_rs, ids_ss, ids_rs, part_ss, part_rs, res_ss, res_rs, ret_ss, ret_rs,
):
    tile, lev = lax.axis_index("tile"), lax.axis_index("lev")
    east, west = lax.rem(tile + 1, NTILE), lax.rem(tile + NTILE - 1, NTILE)
    above, below = lax.rem(lev + 1, NLEV), lax.rem(lev + NLEV - 1, NLEV)

    def remote(src, dst, ss, rs, target):
        return pltpu.make_async_remote_copy(
            src_ref=src, dst_ref=dst, send_sem=ss, recv_sem=rs, device_id=target, device_id_type=MESH
        )

    barrier = pltpu.get_barrier_semaphore()

    def greet_tile(d, carry):
        pl.semaphore_signal(
            barrier, inc=1, device_id={"tile": lax.rem(tile + d, NTILE)}, device_id_type=MESH
        )
        return carry

    def greet_lev(d, carry):
        pl.semaphore_signal(
            barrier, inc=1, device_id={"lev": lax.rem(lev + d, NLEV)}, device_id_type=MESH
        )
        return carry

    lax.fori_loop(1, NTILE, greet_tile, 0)
    lax.fori_loop(1, NLEV, greet_lev, 0)
    loads = [
        pltpu.make_async_copy(conc, x0.at[:, pl.ds(1, LV)], local_sem.at[0]),
        pltpu.make_async_copy(u_in, u, local_sem.at[1]),
        pltpu.make_async_copy(v_in, v, local_sem.at[2]),
        pltpu.make_async_copy(k_in, k.at[pl.ds(1, LV)], local_sem.at[3]),
    ]
    for copy in loads:
        copy.start()

    row8 = lax.broadcasted_iota(jnp.int32, (8, 128), 1) < CAP

    def lev_copies(x, i):
        return [
            remote(x.at[:, LV], x.at[:, 0], halo_ss.at[i, 0], halo_rs.at[i, 0], {"lev": above}),
            remote(x.at[:, 1], x.at[:, LV + 1], halo_ss.at[i, 1], halo_rs.at[i, 1], {"lev": below}),
        ]

    def lon_copies(i):
        return [
            remote(lon_out.at[i, 0], lon_in.at[i, 0], halo_ss.at[i, 2], halo_rs.at[i, 2], {"tile": east}),
            remote(lon_out.at[i, 1], lon_in.at[i, 1], halo_ss.at[i, 3], halo_rs.at[i, 3], {"tile": west}),
        ]

    def stage_lon(x, i):
        for t in range(TR):
            for l in range(LV):
                lon_out[i, 0, t * LV + l : t * LV + l + 1, :] = x[t, l + 1, LON - 1 : LON, :]
                lon_out[i, 1, t * LV + l : t * LV + l + 1, :] = x[t, l + 1, 0:1, :]

    def finish_halo(x, i, copies):
        for copy in copies:
            copy.wait_recv()

        @pl.when(lev == NLEV - 1)
        def _():
            x[:, LV + 1] = jnp.zeros((TR, LON, LAT), F32)

        @pl.when(tile == NTILE - 1)
        def _():
            lon_in[i, 1] = jnp.zeros((24, LAT), F32)

    pl.semaphore_wait(barrier, NTILE - 1 + NLEV - 1)

    for copy in loads:
        copy.wait()
    halo = [lev_copies(x0, 0)]
    k_copy = remote(k.at[LV], k.at[0], halo_ss.at[0, 4], halo_rs.at[0, 4], {"lev": above})
    for copy in halo[0] + [k_copy]:
        copy.start()
    stage_lon(x0, 0)
    for l in range(LV):
        lon_out[0, 0, 18 + l : 19 + l, :] = u[l, LON - 1 : LON, :]
    lons = [lon_copies(0)]
    for copy in lons[0]:
        copy.start()

    target = fields[13:14, :].astype(jnp.int32)
    match = (lax.broadcasted_iota(jnp.int32, (NTILE, SND), 0) == target).astype(F32)
    earlier = (
        lax.broadcasted_iota(jnp.int32, (SND, SND), 0) < lax.broadcasted_iota(jnp.int32, (SND, SND), 1)
    ).astype(F32).astype(BF16)
    before = jnp.dot(match.astype(BF16), earlier, preferred_element_type=F32)
    rank = jnp.sum(before * match, axis=0, keepdims=True).astype(jnp.int32)
    slot = target * CAP + rank
    for i in range(NLEV):
        hot[i * CHUNK : (i + 1) * CHUNK, :] = (
            (lax.broadcasted_iota(jnp.int32, (CHUNK, SND), 0) + i * CHUNK == slot).astype(F32).astype(BF16)
        )
    data = jnp.concatenate([p.astype(F32) for p in parts_of(fields[...], 3)], axis=0).astype(BF16)

    def pack(i, carry):
        rows = pl.ds(pl.multiple_of(i * CHUNK, CHUNK), CHUNK)
        got = lax.dot_general(data, hot[rows, :], NT, preferred_element_type=F32)
        got = got[0:16] + got[16:32] + got[32:48]
        for h in range(2):
            a, b = got[0:8, h * 128 : h * 128 + 128], got[8:16, h * 128 : h * 128 + 128]
            ids_out[i * 4 + h * 2] = jnp.where(row8, a, pltpu.roll(b, CAP, 1))
            ids_out[i * 4 + h * 2 + 1] = jnp.where(row8, pltpu.roll(a, CAP, 1), b)
        return carry

    lax.fori_loop(0, NLEV, pack, 0)
    ids_in[tile] = ids_out[tile]

    def ids_copy(d):
        peer = lax.rem(tile + d, NTILE)
        return remote(ids_out.at[peer], ids_in.at[tile], ids_ss.at[d], ids_rs.at[d], {"tile": peer})

    def ids_wait(d, carry):
        source = lax.rem(tile + NTILE - d, NTILE)
        remote(
            ids_out.at[source], ids_in.at[source], ids_ss.at[d], ids_rs.at[d], {"tile": source}
        ).wait_recv()
        return carry

    def start(make):
        def step(d, carry):
            make(d).start()
            return carry
        return step

    def sent(make):
        def step(d, carry):
            make(d).wait_send()
            return carry
        return step

    lax.fori_loop(1, NTILE, start(ids_copy), 0)

    last_row = lax.broadcasted_iota(jnp.int32, (LON, LAT), 0) == LON - 1
    first_row = lax.broadcasted_iota(jnp.int32, (LON, LAT), 0) == 0
    open_face = lax.broadcasted_iota(jnp.int32, (LON, LAT), 1) < LAT - 1

    def sweep(x, i, adjoint, levels, put):
        for l in levels:
            ul, kl, kb = u[l], k[l + 1], k[l]
            uw = jnp.where(first_row, lon_in[0, 0, 18 + l : 19 + l, :], pltpu.roll(ul, 1, 0))
            vl = jnp.where(open_face, v[l], 0.0)
            a, bw = jnp.maximum(ul, 0.0), jnp.minimum(uw, 0.0)
            p, q = jnp.maximum(vl, 0.0), jnp.minimum(vl, 0.0)
            if adjoint:
                qs = pltpu.roll(q, 1, 1)
            else:
                b, aw = jnp.minimum(ul, 0.0), jnp.maximum(uw, 0.0)
            for t in range(TR):
                r = t * LV + l
                c = x[t, l + 1]
                ce = jnp.where(last_row, lon_in[i, 1, r : r + 1, :], pltpu.roll(c, LON - 1, 0))
                cw = jnp.where(first_row, lon_in[i, 0, r : r + 1, :], pltpu.roll(c, 1, 0))
                cn = pltpu.roll(c, LAT - 1, 1)
                vert = kl * (x[t, l + 2] - c) - kb * (c - x[t, l])
                if adjoint:
                    cs = pltpu.roll(c, 1, 1)
                    y = c + (a * (ce - c) + bw * (c - cw)) + (p * (cn - c) + qs * (c - cs)) + vert
                else:
                    fn = p * c + q * cn
                    y = c - (a * c + b * ce) + (aw * cw + bw * c) - fn + pltpu.roll(fn, 1, 1) + vert
                put(t, l, y)

    def put_in(x):
        def put(t, l, y):
            x[t, l + 1] = y
        return put

    def two_sweeps(first, second, i, adjoint, put):
        sweep(first, i, adjoint, (0, LV - 1), put_in(second))
        halo.append(lev_copies(second, i + 1))
        for copy in halo[-1]:
            copy.start()
        sweep(first, i, adjoint, range(1, LV - 1), put_in(second))
        stage_lon(second, i + 1)
        lons.append(lon_copies(i + 1))
        for copy in lons[-1]:
            copy.start()

    finish_halo(x0, 0, halo[0] + lons[0] + [k_copy])

    @pl.when(lev == 0)
    def _():
        k[0] = jnp.zeros((LON, LAT), F32)

    @pl.when(tile == 0)
    def _():
        lon_in[0, 0, 18:24] = jnp.zeros((6, LAT), F32)

    two_sweeps(x0, x1, 0, False, None)

    lax.fori_loop(1, NTILE, ids_wait, 0)

    def unpack(c, carry):
        left, right = [], []
        for h in range(2):
            a, b = ids_in[c * 4 + h * 2], ids_in[c * 4 + h * 2 + 1]
            left.append(jnp.where(row8, a, pltpu.roll(b, CAP, 1)))
            right.append(jnp.where(row8, pltpu.roll(a, CAP, 1), b))
        ga, gb = jnp.concatenate(left, axis=1), jnp.concatenate(right, axis=1)
        fb[c] = gb
        ga = ga.astype(jnp.int32)
        kind = gb[0:1, :].astype(jnp.int32)
        weights = jnp.zeros((LV, CHUNK), F32)
        for j in range(8):
            weights = weights + jnp.where(kind == j, kern[:, j : j + 1], 0.0)
        kw[c, 0:LV, :] = weights
        for j in range(FOOT):
            cols = slice(j * CHUNK, (j + 1) * CHUNK)
            lat = (lax.broadcasted_iota(jnp.int32, (LAT, CHUNK), 0) == ga[j : j + 1, :]).astype(F32).astype(BF16)
            lathot[c, 0:LAT, cols] = lat
            lathot[c, LAT : 2 * LAT, cols] = lat
            lonhot[c, :, cols] = (
                lax.broadcasted_iota(jnp.int32, (LON, CHUNK), 0) == ga[4 + j : 5 + j, :]
            ).astype(F32)
        return carry

    lax.fori_loop(0, NLEV, unpack, 0)

    finish_halo(x1, 1, halo[1] + lons[1])

    def put_evolved(t, l, y):
        r = (t * LV + l) * LON
        high, low = parts_of(y, 2)
        e[r : r + LON, 0:LAT] = high
        e[r : r + LON, LAT : 2 * LAT] = low

    sweep(x1, 1, False, range(LV), put_evolved)

    def part_copy(d):
        peer = lax.rem(lev + d, NLEV)
        return remote(part_out.at[peer], part_in.at[lev], part_ss.at[d], part_rs.at[d], {"lev": peer})

    def gather(c, carry):
        picked[...] = jnp.dot(e[...], lathot[c], preferred_element_type=F32)
        mask = lonhot[c]
        for t in range(TR):
            acc = jnp.zeros((LON, CHUNK), F32)
            for l in range(LV):
                r = (t * LV + l) * LON
                block = picked[r : r + LON, :] * mask
                block = (block[:, 0:CHUNK] + block[:, CHUNK : 2 * CHUNK]) + (
                    block[:, 2 * CHUNK : 3 * CHUNK] + block[:, 3 * CHUNK :]
                )
                acc = acc + block * kw[c, l : l + 1, :]
            row = jnp.sum(acc, axis=0, keepdims=True)
            part_out[c, t : t + 1, :] = row[:, 0:128]
            part_out[c, 3 + t : 4 + t, :] = row[:, 128:256]
        return carry

    def gather_at(d, carry):
        gather(lax.rem(lev + d, NLEV), 0)
        part_copy(d).start()
        return carry

    lax.fori_loop(1, NLEV, gather_at, 0)
    gather(lev, 0)
    part_in[lev] = part_out[lev]

    def part_wait(d, carry):
        source = lax.rem(lev + NLEV - d, NLEV)
        remote(
            part_out.at[source], part_in.at[source], part_ss.at[d], part_rs.at[d], {"lev": source}
        ).wait_recv()
        return carry

    lax.fori_loop(1, NLEV, part_wait, 0)
    model = part_in[0]
    for z in range(1, NLEV):
        model = model + part_in[z]
    own = fb[lev]
    seen = jnp.concatenate([own[1:4, 0:128], own[1:4, 128:256]], axis=0)
    res[lev, 0:6] = model[0:6] * (1.0 / FOOT) - seen

    def res_copy(d):
        peer = lax.rem(lev + d, NLEV)
        return remote(res.at[lev], res.at[lev], res_ss.at[d], res_rs.at[d], {"lev": peer})

    def res_wait(d):
        source = lax.rem(lev + NLEV - d, NLEV)
        remote(res.at[source], res.at[source], res_ss.at[d], res_rs.at[d], {"lev": source}).wait_recv()

    lax.fori_loop(1, NLEV, start(res_copy), 0)

    def scatter(c):
        mask = lonhot[c]
        for t in range(TR):
            row = jnp.concatenate([res[c, t : t + 1, :], res[c, 3 + t : 4 + t, :]], axis=1)
            row = row * fb[c, 4:5, :] * (1.0 / FOOT)
            for l in range(LV):
                r = (t * LV + l) * LON
                high, low = parts_of(row * kw[c, l : l + 1, :], 2)
                for h, piece in enumerate((high, low)):
                    piece = piece.astype(F32)
                    for j in range(FOOT):
                        cols = slice(j * CHUNK, (j + 1) * CHUNK)
                        terms[h * ROWS + r : h * ROWS + r + LON, cols] = (mask[:, cols] * piece).astype(BF16)
        return lax.dot_general(terms[...], lathot[c, 0:LAT, :], NT, preferred_element_type=F32)

    total[...] = scatter(lev)

    def scatter_at(d, carry):
        res_wait(d)
        total[...] += scatter(lax.rem(lev + NLEV - d, NLEV))
        return carry

    lax.fori_loop(1, NLEV, scatter_at, 0)

    def ret_copy(d):
        peer = lax.rem(tile + d, NTILE)
        return remote(res.at[peer // 4], ret_in.at[tile], ret_ss.at[d], ret_rs.at[d], {"tile": peer})

    def ret_wait(d, carry):
        source = lax.rem(tile + NTILE - d, NTILE)
        remote(
            res.at[source // 4], ret_in.at[source], ret_ss.at[d], ret_rs.at[d], {"tile": source}
        ).wait_recv()
        return carry

    lax.fori_loop(1, NTILE, start(ret_copy), 0)
    ret_in[tile] = res[tile // 4]

    for t in range(TR):
        for l in range(LV):
            r = (t * LV + l) * LON
            x2[t, l + 1] = total[r : r + LON, :] + total[ROWS + r : ROWS + r + LON, :]
    halo.append(lev_copies(x2, 2))
    for copy in halo[2]:
        copy.start()
    stage_lon(x2, 2)
    lons.append(lon_copies(2))
    for copy in lons[2]:
        copy.start()

    lax.fori_loop(1, NTILE, ret_wait, 0)
    pair_odd, odd = lax.rem(tile // 2, 2) == 1, lax.rem(tile, 2) == 1
    for i in range(NTILE // 2):
        halves = []
        for h in range(2):
            got = ret_in[2 * i + h]
            got = jnp.where(pair_odd, pltpu.roll(got, 5, 0), got)
            moved = pltpu.roll(got, CAP, 1)
            halves.append(jnp.where(odd, got, moved) if h else jnp.where(odd, moved, got))
        both = jnp.where(row8, halves[0], halves[1])
        keep = lax.broadcasted_iota(jnp.int32, (8, 128), 0) < TR
        for j, piece in enumerate(parts_of(jnp.where(keep, both, 0.0), 3)):
            spread[j, :, i * 128 : (i + 1) * 128] = piece.astype(F32)
    back = jnp.concatenate([spread[0], spread[1], spread[2], jnp.zeros((8, SLOTS), F32)], axis=0).astype(BF16)
    back = jnp.dot(back, hot[...], preferred_element_type=F32)
    residual[...] = (back[0:8] + back[8:16] + back[16:24])[0:TR]

    finish_halo(x2, 2, halo[2] + lons[2])
    two_sweeps(x2, x3, 2, True, None)
    finish_halo(x3, 3, halo[3] + lons[3])

    def put_gradient(t, l, y):
        gradient[t, l] = y

    sweep(x3, 3, True, range(LV), put_gradient)

    for copies in halo + lons + [[k_copy]]:
        for copy in copies:
            copy.wait_send()
    lax.fori_loop(1, NTILE, sent(ids_copy), 0)
    lax.fori_loop(1, NLEV, sent(part_copy), 0)
    lax.fori_loop(1, NLEV, sent(res_copy), 0)
    lax.fori_loop(1, NTILE, sent(ret_copy), 0)


def body(conc, u_wind, v_wind, mixing, kernels, observed, obs_weight, column_tile, footprint, kernel_index):
    feet = footprint.T
    lon = (feet // LAT).astype(F32)
    lat = (feet % LAT).astype(F32)
    fields = jnp.concatenate(
        [
            lat,
            lon,
            kernel_index[None].astype(F32),
            observed,
            obs_weight[None],
            column_tile.T.astype(F32),
            jnp.zeros((2, SND), F32),
        ],
        axis=0,
    )
    dma = pltpu.SemaphoreType.DMA
    anywhere, vmem = pl.BlockSpec(memory_space=pl.ANY), pl.BlockSpec(memory_space=pltpu.VMEM)
    ext = pltpu.VMEM((TR, LV + 2, LON, LAT), F32)
    return pl.pallas_call(
        kernel,
        out_shape=(
            jax.ShapeDtypeStruct((TR, SND), F32),
            jax.ShapeDtypeStruct((TR, LV, LON, LAT), F32),
        ),
        in_specs=[anywhere] * 4 + [vmem] * 2,
        out_specs=(vmem, vmem),
        scratch_shapes=[
            ext, ext, ext, ext,
            pltpu.VMEM((LV, LON, LAT), F32),
            pltpu.VMEM((LV, LON, LAT), F32),
            pltpu.VMEM((LV + 1, LON, LAT), F32),
            pltpu.VMEM((4, 2, 24, LAT), F32),
            pltpu.VMEM((4, 2, 24, LAT), F32),
            pltpu.VMEM((NTILE, 8, 128), F32),
            pltpu.VMEM((NTILE, 8, 128), F32),
            pltpu.VMEM((SLOTS, SND), BF16),
            pltpu.VMEM((NLEV, 8, CHUNK), F32),
            pltpu.VMEM((NLEV, 8, CHUNK), F32),
            pltpu.VMEM((NLEV, 8, CHUNK), F32),
            pltpu.VMEM((NLEV, 2 * LAT, LOOK), BF16),
            pltpu.VMEM((NLEV, LON, LOOK), F32),
            pltpu.VMEM((3, 8, SLOTS), F32),
            pltpu.VMEM((ROWS, 2 * LAT), BF16),
            pltpu.VMEM((ROWS, LOOK), F32),
            pltpu.VMEM((NLEV, 8, 128), F32),
            pltpu.VMEM((NLEV, 8, 128), F32),
            pltpu.VMEM((NLEV, 8, 128), F32),
            pltpu.VMEM((NTILE, 8, 128), F32),
            pltpu.VMEM((2 * ROWS, LOOK), BF16),
            pltpu.VMEM((2 * ROWS, LAT), F32),
            dma((4,)),
            dma((4, 5)), dma((4, 5)),
            dma((NTILE,)), dma((NTILE,)),
            dma((NLEV,)), dma((NLEV,)),
            dma((NLEV,)), dma((NLEV,)),
            dma((NTILE,)), dma((NTILE,)),
        ],
        compiler_params=pltpu.CompilerParams(
            collective_id=0, has_side_effects=True, vmem_limit_bytes=56 * 1024 * 1024
        ),
    )(conc, u_wind, v_wind, mixing, kernels.T, fields)


def solution(mesh):
    placed = (
        P(None, "lev", "tile", None),
        P("lev", "tile", None),
        P("lev", "tile", None),
        P("lev", "tile", None),
        P(None, "lev"),
        P(None, "tile"),
        P("tile"),
        P("tile", None),
        P("tile", None),
        P("tile"),
    )
    return jax.shard_map(
        body,
        mesh=mesh,
        in_specs=placed,
        out_specs=(P(None, "tile"), P(None, "lev", "tile", None)),
        check_vma=False,
    )
```

```python
import jax
import jax.numpy as jnp
from jax import lax
from jax.experimental import pallas as pl
from jax.experimental.pallas import tpu as pltpu
from jax.sharding import PartitionSpec as P

MESH = pl.DeviceIdType.MESH
F32, BF16, I32 = jnp.float32, jnp.bfloat16, jnp.int32
NT = (((1,), (1,)), ((), ()))
TR, LV, LON, LAT, KIND = 3, 6, 32, 384, 8
EXT = LV + 4
ROWS = TR * KIND * LON
PER = KIND * LON
NTILE, NLEV, CAP, SND, FOOT = 32, 8, 64, 1024, 4
SLOTS = NTILE * CAP
CHUNK = SLOTS // NLEV
LOOK = FOOT * CHUNK


def parts_of(x, count):
    pieces = []
    for _ in range(count):
        piece = x.astype(BF16)
        pieces.append(piece)
        x = x - piece.astype(F32)
    return pieces


def onehot(rows, index, base=0):
    shape = (rows, index.shape[1])
    return (lax.broadcasted_iota(I32, shape, 0) + base == index).astype(F32)


def loop(low, high, body):
    def step(i, carry):
        body(i)
        return carry

    lax.fori_loop(low, high, step, 0)


def kernel(
    conc, u_in, v_in, k_in, kern, observed, weight, column, feet, kinds,
    residual, gradient,
    x0, x1, x2, x3, u, v, k, lon_out, lon_in, kern_all, kern_wide, fields,
    ids_out, ids_in, hot, fb, kindhot, lathot, lonhot, lonbits, spread,
    e, picked, part_out, part_in, res, ret_in, terms, total,
    local_sem, lev_ss, lev_rs, lon_ss, lon_rs, ids_ss, ids_rs, part_ss, part_rs, ret_ss, ret_rs,
):
    tile, lev = lax.axis_index("tile"), lax.axis_index("lev")
    east, west = lax.rem(tile + 1, NTILE), lax.rem(tile + NTILE - 1, NTILE)
    above, below = lax.rem(lev + 1, NLEV), lax.rem(lev + NLEV - 1, NLEV)

    def remote(src, dst, ss, rs, target):
        return pltpu.make_async_remote_copy(
            src_ref=src, dst_ref=dst, send_sem=ss, recv_sem=rs, device_id=target, device_id_type=MESH
        )

    barrier = pltpu.get_barrier_semaphore()

    def greet(target):
        pl.semaphore_signal(barrier, inc=1, device_id=target, device_id_type=MESH)

    loop(1, NLEV, lambda d: greet({"lev": lax.rem(lev + d, NLEV)}))
    loop(1, NTILE, lambda d: greet({"tile": lax.rem(tile + d, NTILE)}))
    own = pl.ds(2, LV)
    loads = [
        pltpu.make_async_copy(conc, x0.at[:, own], local_sem.at[0]),
        pltpu.make_async_copy(u_in, u.at[pl.ds(1, LV)], local_sem.at[1]),
        pltpu.make_async_copy(v_in, v.at[pl.ds(1, LV)], local_sem.at[2]),
        pltpu.make_async_copy(k_in, k.at[own], local_sem.at[3]),
    ]
    for copy in loads:
        copy.start()

    half = lax.broadcasted_iota(I32, (8, 128), 1) < CAP

    foot = feet[...]
    foot_lon = lax.shift_right_logical(lax.shift_right_logical(foot, 7) * 171, 9)
    fields[0:4, :] = (foot - foot_lon * LAT).astype(F32)
    fields[4:8, :] = foot_lon.astype(F32)
    fields[8:9, :] = kinds[...].astype(F32)
    fields[9:12, :] = observed[...]
    fields[12:13, :] = weight[...]
    fields[13:16, :] = jnp.zeros((3, SND), F32)
    target = column[...]
    match = onehot(NTILE, target)
    earlier = (
        lax.broadcasted_iota(I32, (SND, SND), 0) < lax.broadcasted_iota(I32, (SND, SND), 1)
    ).astype(F32).astype(BF16)
    before = jnp.dot(match.astype(BF16), earlier, preferred_element_type=F32)
    slot = target * CAP + jnp.sum(before * match, axis=0, keepdims=True).astype(I32)
    data = jnp.concatenate([p.astype(F32) for p in parts_of(fields[...], 3)], axis=0).astype(BF16)

    def pack(i):
        rows = pl.ds(pl.multiple_of(i * CHUNK, CHUNK), CHUNK)
        hot[rows, :] = onehot(CHUNK, slot, i * CHUNK).astype(BF16)
        got = lax.dot_general(data, hot[rows, :], NT, preferred_element_type=F32)
        got = got[0:16] + got[16:32] + got[32:48]
        for h in range(2):
            a, b = got[0:8, h * 128 : h * 128 + 128], got[8:16, h * 128 : h * 128 + 128]
            ids_out[i * 4 + h * 2] = jnp.where(half, a, pltpu.roll(b, CAP, 1))
            ids_out[i * 4 + h * 2 + 1] = jnp.where(half, pltpu.roll(a, CAP, 1), b)

    loop(0, NLEV, pack)
    ids_in[tile] = ids_out[tile]
    kern_all[0, :, 0:LV] = kern[...]

    blank = jnp.zeros((TR, LON, LAT), F32)
    x0[:, 1], x0[:, 8] = blank, blank
    x1[:, 0], x1[:, 9] = blank, blank

    def lon_copies(i):
        return [
            remote(lon_out.at[i, 0], lon_in.at[i, 0], lon_ss.at[i, 0], lon_rs.at[i, 0], {"tile": east}),
            remote(lon_out.at[i, 1], lon_in.at[i, 1], lon_ss.at[i, 1], lon_rs.at[i, 1], {"tile": west}),
        ]

    def stage_lon(x, i, low, high):
        def one(n):
            for t in range(TR):
                lon_out[i, 0, t * 8 + n - 1] = x[t, n, LON - 1]
                lon_out[i, 1, t * 8 + n - 1] = x[t, n, 0]
            if i < 2:
                lon_out[i, 0, 23 + n] = u[n - 1, LON - 1]

        loop(low, high, one)

    def finish_lon(i):
        for copy in lons[i]:
            copy.wait_recv()

        @pl.when(tile == NTILE - 1)
        def _():
            lon_in[i, 1] = jnp.zeros((32, LAT), F32)

        if i < 2:

            @pl.when(tile == 0)
            def _():
                lon_in[i, 0, 24:32] = jnp.zeros((8, LAT), F32)

    for copy in loads:
        copy.wait()
    stage_lon(x0, 0, 2, 8)

    lev_moves = [
        (k.at[pl.ds(LV, 2)], k.at[pl.ds(0, 2)], above),
        (kern_all.at[0], kern_all.at[1], above),
        (kern_all.at[0], kern_all.at[2], below),
        (u.at[LV], u.at[0], above),
        (u.at[1], u.at[LV + 1], below),
        (v.at[LV], v.at[0], above),
        (v.at[1], v.at[LV + 1], below),
        (k.at[2], k.at[LV + 2], below),
    ]
    lev_copies = [
        remote(src, dst, lev_ss.at[n], lev_rs.at[n], {"lev": to}) for n, (src, dst, to) in enumerate(lev_moves)
    ]
    lons = [lon_copies(0)]

    def ids_copy(d):
        peer = lax.rem(tile + d, NTILE)
        return remote(ids_out.at[peer], ids_in.at[tile], ids_ss.at[d], ids_rs.at[d], {"tile": peer})

    def ids_wait(d):
        source = lax.rem(tile + NTILE - d, NTILE)
        remote(ids_out.at[source], ids_in.at[source], ids_ss.at[d], ids_rs.at[d], {"tile": source}).wait_recv()

    pl.semaphore_wait(barrier, NTILE - 1 + NLEV - 1)
    for copy in lons[0] + lev_copies:
        copy.start()
    loop(1, NTILE, lambda d: ids_copy(d).start())

    last_row = lax.broadcasted_iota(I32, (LON, LAT), 0) == LON - 1
    first_row = lax.broadcasted_iota(I32, (LON, LAT), 0) == 0
    open_face = lax.broadcasted_iota(I32, (LON, LAT), 1) < LAT - 1

    def sweep(x, i, adjoint, low, high, put):
        def one(n):
            ul, kl, kb = u[n - 1], k[n], k[n - 1]
            uw = jnp.where(first_row, lon_in[min(i, 1), 0, pl.ds(23 + n, 1), :], pltpu.roll(ul, 1, 0))
            vl = jnp.where(open_face, v[n - 1], 0.0)
            a, bw = jnp.maximum(ul, 0.0), jnp.minimum(uw, 0.0)
            p, q = jnp.maximum(vl, 0.0), jnp.minimum(vl, 0.0)
            if adjoint:
                qs = pltpu.roll(q, 1, 1)
            else:
                b, aw = jnp.minimum(ul, 0.0), jnp.maximum(uw, 0.0)
            for t in range(TR):
                row = pl.ds(t * 8 + n - 1, 1)
                c = x[t, n]
                ce = jnp.where(last_row, lon_in[i, 1, row, :], pltpu.roll(c, LON - 1, 0))
                cw = jnp.where(first_row, lon_in[i, 0, row, :], pltpu.roll(c, 1, 0))
                cn = pltpu.roll(c, LAT - 1, 1)
                vert = kl * (x[t, n + 1] - c) - kb * (c - x[t, n - 1])
                if adjoint:
                    cs = pltpu.roll(c, 1, 1)
                    y = c + (a * (ce - c) + bw * (c - cw)) + (p * (cn - c) + qs * (c - cs)) + vert
                else:
                    fn = p * c + q * cn
                    y = c - (a * c + b * ce) + (aw * cw + bw * c) - fn + pltpu.roll(fn, 1, 1) + vert
                put(t, n, y)

        loop(low, high, one)

    def put_in(x):
        def put(t, n, y):
            x[t, n] = y

        return put

    lev_copies[0].wait_recv()

    @pl.when(lev == 0)
    def _():
        k[0:2] = jnp.zeros((2, LON, LAT), F32)

    finish_lon(0)
    sweep(x0, 0, False, 2, 8, put_in(x1))
    for t in range(TR):
        x1[t, 1] = k[1] * x0[t, 2]
        x1[t, 8] = k[7] * x0[t, 7]

    @pl.when(lev == NLEV - 1)
    def _():
        x1[:, 8] = blank

    for copy in lev_copies[1:]:
        copy.wait_recv()
    stage_lon(x1, 1, 1, 9)
    lons.append(lon_copies(1))
    for copy in lons[1]:
        copy.start()

    @pl.when(lev == 0)
    def _():
        kern_all[1] = jnp.zeros((KIND, 128), F32)

    @pl.when(lev == NLEV - 1)
    def _():
        kern_all[2] = jnp.zeros((KIND, 128), F32)

    for n in range(EXT):
        which, col = (1, 4 + n) if n < 2 else (0, n - 2) if n < 8 else (2, n - 8)
        kern_wide[n] = jnp.broadcast_to(kern_all[which, :, col : col + 1], (KIND, 128))

    loop(1, NTILE, ids_wait)

    def unpack(c):
        left, right = [], []
        for h in range(2):
            a, b = ids_in[c * 4 + h * 2], ids_in[c * 4 + h * 2 + 1]
            left.append(jnp.where(half, a, pltpu.roll(b, CAP, 1)))
            right.append(jnp.where(half, pltpu.roll(a, CAP, 1), b))
        ga, gb = jnp.concatenate(left, axis=1), jnp.concatenate(right, axis=1)
        fb[c] = gb
        ga = ga.astype(I32)
        kindhot[c] = onehot(KIND, gb[0:1, :].astype(I32))
        for j in range(FOOT):
            cols = slice(j * CHUNK, (j + 1) * CHUNK)
            lat = onehot(LAT, ga[j : j + 1, :]).astype(BF16)
            lathot[c, 0:LAT, cols] = lat
            lathot[c, LAT : 2 * LAT, cols] = lat
            lon = onehot(LON, ga[4 + j : 5 + j, :])
            lonhot[c, :, cols] = lon
            lonbits[c, :, cols] = lon.astype(BF16)

    loop(0, NLEV, unpack)

    finish_lon(1)
    sweep(x1, 1, False, 1, 9, put_in(x2))
    for t in range(TR):
        x2[t, 0] = k[0] * x1[t, 1]
        x2[t, 9] = k[8] * x1[t, 8]

    def profile(i):
        t, h = i // 2, lax.rem(i, 2)
        rows = pl.ds(pl.multiple_of(h * 16, 16), 16)
        for w in range(LAT // 128):
            cols = slice(w * 128, (w + 1) * 128)
            planes = [x2[t, n, rows, cols] for n in range(EXT)]
            for j in range(KIND):
                acc = planes[0] * kern_wide[0, j : j + 1, :]
                for n in range(1, EXT):
                    acc = acc + planes[n] * kern_wide[n, j : j + 1, :]
                high, low = parts_of(acc, 2)
                to = pl.ds(pl.multiple_of(t * PER + j * LON + h * 16, 16), 16)
                e[to, cols] = high
                e[to, LAT + w * 128 : LAT + (w + 1) * 128] = low

    loop(0, 2 * TR, profile)

    def part_copy(c, d):
        peer = lax.rem(lev + d, NLEV)
        return remote(part_out.at[c], part_in.at[lev, c], part_ss.at[c, d], part_rs.at[c, d], {"lev": peer})

    def part_wait(c, d):
        source = lax.rem(lev + NLEV - d, NLEV)
        remote(
            part_out.at[c], part_in.at[source, c], part_ss.at[c, d], part_rs.at[c, d], {"lev": source}
        ).wait_recv()

    def gather(c):
        picked[...] = jnp.dot(e[...], lathot[c], preferred_element_type=F32)
        mask = lonhot[c]
        for t in range(TR):
            acc = jnp.zeros((LON, CHUNK), F32)
            for j in range(KIND):
                r = t * PER + j * LON
                block = picked[r : r + LON, :] * mask
                block = (block[:, 0:CHUNK] + block[:, CHUNK : 2 * CHUNK]) + (
                    block[:, 2 * CHUNK : 3 * CHUNK] + block[:, 3 * CHUNK :]
                )
                acc = acc + block * kindhot[c, j : j + 1, :]
            row = jnp.sum(acc, axis=0, keepdims=True)
            part_out[c, t : t + 1, :] = row[:, 0:128]
            part_out[c, 3 + t : 4 + t, :] = row[:, 128:256]
        part_in[lev, c] = part_out[c]
        for d in range(1, NLEV):
            part_copy(c, d).start()

    loop(0, NLEV, gather)

    def ret_copy(peer):
        d = lax.rem(peer + NTILE - tile, NTILE)
        return remote(res.at[peer // 4], ret_in.at[tile], ret_ss.at[d], ret_rs.at[d], {"tile": peer})

    def ret_wait(d):
        source = lax.rem(tile + NTILE - d, NTILE)
        remote(res.at[source // 4], ret_in.at[source], ret_ss.at[d], ret_rs.at[d], {"tile": source}).wait_recv()

    total[...] = jnp.zeros((ROWS, LAT), F32)

    def scatter(c):
        for d in range(1, NLEV):
            part_wait(c, d)
        model = part_in[0, c]
        for z in range(1, NLEV):
            model = model + part_in[z, c]
        seen = jnp.concatenate([fb[c, 1:4, 0:128], fb[c, 1:4, 128:256]], axis=0)
        res[c, 0:6] = model[0:6] * (1.0 / FOOT) - seen
        for n in range(4):
            peer = c * 4 + n

            @pl.when(peer != tile)
            def _():
                ret_copy(peer).start()

        mask = lonbits[c]
        for t in range(TR):
            row = jnp.concatenate([res[c, t : t + 1, :], res[c, 3 + t : 4 + t, :]], axis=1)
            row = row * fb[c, 4:5, :] * (1.0 / FOOT)
            for h, piece in enumerate(parts_of(row, 2)):
                piece = piece.astype(F32)
                for j in range(KIND):
                    value = jnp.broadcast_to(piece * kindhot[c, j : j + 1, :], (16, CHUNK)).astype(BF16)
                    value = jnp.concatenate([value] * FOOT, axis=1)
                    r = h * PER + j * LON
                    terms[t, r : r + 16, :] = mask[0:16] * value
                    terms[t, r + 16 : r + 32, :] = mask[16:32] * value
            got = lax.dot_general(terms[t], lathot[c, 0:LAT, :], NT, preferred_element_type=F32)
            total[t * PER : (t + 1) * PER, :] += got[0:PER] + got[PER:]

    loop(0, NLEV, scatter)
    ret_in[tile] = res[tile // 4]

    def force(i):
        t, h = i // 4, lax.rem(i, 4)
        rows = pl.ds(pl.multiple_of(h * 8, 8), 8)
        for w in range(LAT // 128):
            cols = slice(w * 128, (w + 1) * 128)
            sums = [
                total[pl.ds(pl.multiple_of(t * PER + j * LON + h * 8, 8), 8), cols] for j in range(KIND)
            ]
            for n in range(EXT):
                acc = sums[0] * kern_wide[n, 0:1, :]
                for j in range(1, KIND):
                    acc = acc + sums[j] * kern_wide[n, j : j + 1, :]
                x2[t, n, rows, cols] = acc

    loop(0, 4 * TR, force)
    stage_lon(x2, 2, 1, 9)
    lons.append(lon_copies(2))
    for copy in lons[2]:
        copy.start()

    loop(1, NTILE, ret_wait)
    pair_odd, odd = lax.rem(tile // 2, 2) == 1, lax.rem(tile, 2) == 1
    keep = lax.broadcasted_iota(I32, (8, 128), 0) < TR

    def regroup(i):
        halves = []
        for h in range(2):
            got = ret_in[2 * i + h]
            got = jnp.where(pair_odd, pltpu.roll(got, 5, 0), got)
            moved = pltpu.roll(got, CAP, 1)
            halves.append(jnp.where(odd, got, moved) if h else jnp.where(odd, moved, got))
        both = jnp.where(half, halves[0], halves[1])
        cols = pl.ds(pl.multiple_of(i * 128, 128), 128)
        for j, piece in enumerate(parts_of(jnp.where(keep, both, 0.0), 3)):
            spread[j * 8 : j * 8 + 8, cols] = piece.astype(F32)

    loop(0, NTILE // 2, regroup)
    back = jnp.concatenate([spread[...], jnp.zeros((8, SLOTS), F32)], axis=0).astype(BF16)
    back = jnp.dot(back, hot[...], preferred_element_type=F32)
    residual[...] = (back[0:8] + back[8:16] + back[16:24])[0:TR]

    finish_lon(2)
    sweep(x2, 2, True, 1, 9, put_in(x3))

    @pl.when(lev == NLEV - 1)
    def _():
        x3[:, 8] = blank

    stage_lon(x3, 3, 2, 8)
    lons.append(lon_copies(3))
    for copy in lons[3]:
        copy.start()
    finish_lon(3)

    def put_gradient(t, n, y):
        gradient[t, n - 2] = y

    sweep(x3, 3, True, 2, 8, put_gradient)

    for copies in lons + [lev_copies]:
        for copy in copies:
            copy.wait_send()
    loop(1, NTILE, lambda d: ids_copy(d).wait_send())
    loop(1, NTILE, lambda d: ret_copy(lax.rem(tile + d, NTILE)).wait_send())

    def parts_sent(c):
        for d in range(1, NLEV):
            part_copy(c, d).wait_send()

    loop(0, NLEV, parts_sent)


def store(a, b, a_out, b_out, sem):
    copies = [pltpu.make_async_copy(a, a_out, sem.at[0]), pltpu.make_async_copy(b, b_out, sem.at[1])]
    for copy in copies:
        copy.start()
    for copy in copies:
        copy.wait()


def body(conc, u_wind, v_wind, mixing, kernels, observed, obs_weight, column_tile, footprint, kernel_index):
    dma = pltpu.SemaphoreType.DMA
    anywhere, vmem = pl.BlockSpec(memory_space=pl.ANY), pl.BlockSpec(memory_space=pltpu.VMEM)
    ext = pltpu.VMEM((TR, EXT, LON, LAT), F32)
    shapes = (
        jax.ShapeDtypeStruct((TR, SND), F32),
        jax.ShapeDtypeStruct((TR, LV, LON, LAT), F32),
    )
    found = pl.pallas_call(
        kernel,
        out_shape=shapes,
        in_specs=[anywhere] * 4 + [vmem] * 6,
        out_specs=(vmem, vmem),
        scratch_shapes=[
            ext, ext, ext, ext,
            pltpu.VMEM((LV + 2, LON, LAT), F32),
            pltpu.VMEM((LV + 2, LON, LAT), F32),
            pltpu.VMEM((LV + 3, LON, LAT), F32),
            pltpu.VMEM((4, 2, 32, LAT), F32),
            pltpu.VMEM((4, 2, 32, LAT), F32),
            pltpu.VMEM((3, KIND, 128), F32),
            pltpu.VMEM((EXT, KIND, 128), F32),
            pltpu.VMEM((16, SND), F32),
            pltpu.VMEM((NTILE, 8, 128), F32),
            pltpu.VMEM((NTILE, 8, 128), F32),
            pltpu.VMEM((SLOTS, SND), BF16),
            pltpu.VMEM((NLEV, 8, CHUNK), F32),
            pltpu.VMEM((NLEV, KIND, CHUNK), F32),
            pltpu.VMEM((NLEV, 2 * LAT, LOOK), BF16),
            pltpu.VMEM((NLEV, LON, LOOK), F32),
            pltpu.VMEM((NLEV, LON, LOOK), BF16),
            pltpu.VMEM((24, SLOTS), F32),
            pltpu.VMEM((ROWS, 2 * LAT), BF16),
            pltpu.VMEM((ROWS, LOOK), F32),
            pltpu.VMEM((NLEV, 8, 128), F32),
            pltpu.VMEM((NLEV, NLEV, 8, 128), F32),
            pltpu.VMEM((NLEV, 8, 128), F32),
            pltpu.VMEM((NTILE, 8, 128), F32),
            pltpu.VMEM((TR, 2 * PER, LOOK), BF16),
            pltpu.VMEM((ROWS, LAT), F32),
            dma((4,)),
            dma((8,)), dma((8,)),
            dma((4, 2)), dma((4, 2)),
            dma((NTILE,)), dma((NTILE,)),
            dma((NLEV, NLEV)), dma((NLEV, NLEV)),
            dma((NTILE,)), dma((NTILE,)),
        ],
        compiler_params=pltpu.CompilerParams(
            collective_id=0, has_side_effects=True, vmem_limit_bytes=48 * 1024 * 1024
        ),
    )(
        conc, u_wind, v_wind, mixing, kernels, observed, obs_weight[None], column_tile.T, footprint.T, kernel_index[None]
    )
    return pl.pallas_call(
        store,
        out_shape=shapes,
        in_specs=[anywhere] * 2,
        out_specs=(anywhere, anywhere),
        scratch_shapes=[dma((2,))],
    )(*found)


def solution(mesh):
    placed = (
        P(None, "lev", "tile", None),
        P("lev", "tile", None),
        P("lev", "tile", None),
        P("lev", "tile", None),
        P(None, "lev"),
        P(None, "tile"),
        P("tile"),
        P("tile", None),
        P("tile", None),
        P("tile"),
    )
    return jax.shard_map(
        body,
        mesh=mesh,
        in_specs=placed,
        out_specs=(P(None, "tile"), P(None, "lev", "tile", None)),
        check_vma=False,
    )
```

```python
import jax
import jax.numpy as jnp
from jax import lax
from jax.experimental import pallas as pl
from jax.experimental.pallas import tpu as pltpu
from jax.sharding import PartitionSpec as P

MESH = pl.DeviceIdType.MESH
F32, BF16, I32 = jnp.float32, jnp.bfloat16, jnp.int32
NT = (((1,), (1,)), ((), ()))
TR, LV, LON, LAT, KIND = 3, 6, 32, 384, 8
EXT = LV + 4
ROWS = TR * KIND * LON
PER = KIND * LON
NTILE, NLEV, CAP, SND, FOOT = 32, 8, 64, 1024, 4
SLOTS = NTILE * CAP
CHUNK = SLOTS // NLEV
LOOK = FOOT * CHUNK


def parts_of(x, count):
    pieces = []
    for _ in range(count):
        piece = x.astype(BF16)
        pieces.append(piece)
        x = x - piece.astype(F32)
    return pieces


def onehot(rows, index, base=0):
    shape = (rows, index.shape[1])
    return (lax.broadcasted_iota(I32, shape, 0) + base == index).astype(F32)


def loop(low, high, body):
    def step(i, carry):
        body(i)
        return carry

    lax.fori_loop(low, high, step, 0)


def kernel(
    conc, u_in, v_in, k_in, kern_in, observed_in, weight_in, column_in, feet_in, kinds_in,
    residual, gradient,
    kern, observed, weight, column, feet, kinds, x0, x1, x2, x3, u, v, k, lon_out, lon_in, edge_u, diag_in, edge_y, kern_all, kern_wide, fields,
    ids_out, ids_in, hot, fb, kindhot, lathot, lonhot, lonbits, spread,
    e, picked, part_out, part_in, res, ret_in, terms, total,
    local_sem, lev_ss, lev_rs, diag_ss, diag_rs, lon_ss, lon_rs, ids_ss, ids_rs, part_ss, part_rs, ret_ss, ret_rs,
):
    tile, lev = lax.axis_index("tile"), lax.axis_index("lev")
    east, west = lax.rem(tile + 1, NTILE), lax.rem(tile + NTILE - 1, NTILE)
    above, below = lax.rem(lev + 1, NLEV), lax.rem(lev + NLEV - 1, NLEV)

    def remote(src, dst, ss, rs, target):
        return pltpu.make_async_remote_copy(
            src_ref=src, dst_ref=dst, send_sem=ss, recv_sem=rs, device_id=target, device_id_type=MESH
        )

    barrier = pltpu.get_barrier_semaphore()

    def greet(target):
        pl.semaphore_signal(barrier, inc=1, device_id=target, device_id_type=MESH)

    own = pl.ds(2, LV)
    loads = [
        pltpu.make_async_copy(conc, x0.at[:, own], local_sem.at[0]),
        pltpu.make_async_copy(u_in, u.at[pl.ds(1, LV)], local_sem.at[1]),
        pltpu.make_async_copy(v_in, v.at[pl.ds(1, LV)], local_sem.at[2]),
        pltpu.make_async_copy(k_in, k.at[own], local_sem.at[3]),
    ]
    small = [(kern_in, kern), (observed_in, observed), (weight_in, weight), (column_in, column), (feet_in, feet), (kinds_in, kinds)]
    smalls = [pltpu.make_async_copy(src, dst, local_sem.at[4 + n]) for n, (src, dst) in enumerate(small)]
    for copy in smalls + loads:
        copy.start()
    loop(1, NLEV, lambda d: greet({"lev": lax.rem(lev + d, NLEV)}))
    loop(1, NTILE, lambda d: greet({"tile": lax.rem(tile + d, NTILE)}))
    greet({"tile": west, "lev": below})
    greet({"tile": west, "lev": above})
    for copy in smalls:
        copy.wait()

    half = lax.broadcasted_iota(I32, (8, 128), 1) < CAP

    foot = feet[...]
    foot_lon = lax.shift_right_logical(lax.shift_right_logical(foot, 7) * 171, 9)
    fields[0:4, :] = (foot - foot_lon * LAT).astype(F32)
    fields[4:8, :] = foot_lon.astype(F32)
    fields[8:9, :] = kinds[...].astype(F32)
    fields[9:12, :] = observed[...]
    fields[12:13, :] = weight[...]
    fields[13:16, :] = jnp.zeros((3, SND), F32)
    target = column[...]
    match = onehot(NTILE, target)
    earlier = (
        lax.broadcasted_iota(I32, (SND, SND), 0) < lax.broadcasted_iota(I32, (SND, SND), 1)
    ).astype(F32).astype(BF16)
    before = jnp.dot(match.astype(BF16), earlier, preferred_element_type=F32)
    slot = target * CAP + jnp.sum(before * match, axis=0, keepdims=True).astype(I32)
    data = jnp.concatenate([p.astype(F32) for p in parts_of(fields[...], 3)], axis=0).astype(BF16)

    def pack(i):
        rows = pl.ds(pl.multiple_of(i * CHUNK, CHUNK), CHUNK)
        hot[rows, :] = onehot(CHUNK, slot, i * CHUNK).astype(BF16)
        got = lax.dot_general(data, hot[rows, :], NT, preferred_element_type=F32)
        got = got[0:16] + got[16:32] + got[32:48]
        for h in range(2):
            a, b = got[0:8, h * 128 : h * 128 + 128], got[8:16, h * 128 : h * 128 + 128]
            ids_out[i * 4 + h * 2] = jnp.where(half, a, pltpu.roll(b, CAP, 1))
            ids_out[i * 4 + h * 2 + 1] = jnp.where(half, pltpu.roll(a, CAP, 1), b)

    loop(0, NLEV, pack)
    ids_in[tile] = ids_out[tile]
    kern_all[0, :, 0:LV] = kern[...]

    blank = jnp.zeros((TR, LON, LAT), F32)
    x0[:, 1], x0[:, 8] = blank, blank
    x1[:, 0], x1[:, 9] = blank, blank

    def lon_copies(i):
        rows = pl.ds(0, 48 if i else 32)
        return [
            remote(
                lon_out.at[i, side, rows], lon_in.at[i, side, rows], lon_ss.at[i, side], lon_rs.at[i, side], {"tile": to}
            )
            for side, to in enumerate((east, west))
        ]

    def stage_lon(x, i, low, high):
        def one(n):
            for t in range(TR):
                lon_out[i, 0, t * 8 + n - 1] = x[t, n, LON - 1]
                lon_out[i, 1, t * 8 + n - 1] = x[t, n, 0]
                if i == 2:
                    lon_out[i, 0, 23 + t * 8 + n] = x[t, n, LON - 2]
                    lon_out[i, 1, 23 + t * 8 + n] = x[t, n, 1]
            if i == 0:
                lon_out[i, 0, 23 + n] = u[n - 1, LON - 1]

        loop(low, high, one)

    def stage_winds(n):
        lon_out[1, 0, 23 + n] = u[n - 1, LON - 2]
        lon_out[1, 1, 23 + n] = u[n - 1, 0]
        lon_out[1, 0, 31 + n] = v[n - 1, LON - 1]
        lon_out[1, 1, 31 + n] = v[n - 1, 0]
        lon_out[1, 0, 39 + n] = k[n, LON - 1]
        lon_out[1, 1, 39 + n] = k[n, 0]

    def finish_lon(i):
        for copy in lons[i]:
            copy.wait_recv()

        @pl.when(tile == NTILE - 1)
        def _():
            lon_in[i, 1] = jnp.zeros((48, LAT), F32)

    for copy in loads:
        copy.wait()
    stage_lon(x0, 0, 2, 8)

    lev_moves = [
        (k.at[pl.ds(LV, 2)], k.at[pl.ds(0, 2)], above),
        (kern_all.at[0], kern_all.at[1], above),
        (kern_all.at[0], kern_all.at[2], below),
        (u.at[LV], u.at[0], above),
        (u.at[1], u.at[LV + 1], below),
        (v.at[LV], v.at[0], above),
        (v.at[1], v.at[LV + 1], below),
        (k.at[2], k.at[LV + 2], below),
    ]
    lev_copies = [
        remote(src, dst, lev_ss.at[n], lev_rs.at[n], {"lev": to}) for n, (src, dst, to) in enumerate(lev_moves)
    ]
    lons = [lon_copies(0)]
    diag_copies = [
        remote(
            lon_out.at[0, 0, pl.ds(24, 8)], diag_in.at[n], diag_ss.at[n], diag_rs.at[n], {"tile": east, "lev": to}
        )
        for n, to in enumerate((above, below))
    ]

    def ids_copy(d):
        peer = lax.rem(tile + d, NTILE)
        return remote(ids_out.at[peer], ids_in.at[tile], ids_ss.at[d], ids_rs.at[d], {"tile": peer})

    def ids_wait(d):
        source = lax.rem(tile + NTILE - d, NTILE)
        remote(ids_out.at[source], ids_in.at[source], ids_ss.at[d], ids_rs.at[d], {"tile": source}).wait_recv()

    pl.semaphore_wait(barrier, NTILE - 1 + NLEV - 1 + 2)
    for copy in lons[0] + lev_copies[0:1]:
        copy.start()
    loop(1, NTILE, lambda d: ids_copy(d).start())
    for copy in diag_copies + lev_copies[1:]:
        copy.start()

    last_row = lax.broadcasted_iota(I32, (LON, LAT), 0) == LON - 1
    first_row = lax.broadcasted_iota(I32, (LON, LAT), 0) == 0
    open_face = lax.broadcasted_iota(I32, (LON, LAT), 1) < LAT - 1

    def sweep(x, i, adjoint, low, high, put):
        def one(n):
            ul, kl, kb = u[n - 1], k[n], k[n - 1]
            uw = jnp.where(first_row, edge_u[pl.ds(n - 1, 1), :], pltpu.roll(ul, 1, 0))
            vl = jnp.where(open_face, v[n - 1], 0.0)
            a, bw = jnp.maximum(ul, 0.0), jnp.minimum(uw, 0.0)
            p, q = jnp.maximum(vl, 0.0), jnp.minimum(vl, 0.0)
            if adjoint:
                qs = pltpu.roll(q, 1, 1)
            else:
                b, aw = jnp.minimum(ul, 0.0), jnp.maximum(uw, 0.0)
            for t in range(TR):
                row = pl.ds(t * 8 + n - 1, 1)
                c = x[t, n]
                edge_w, edge_e = (lon_in[i, 0, row, :], lon_in[i, 1, row, :]) if i < 3 else (edge_y[0, row, :], edge_y[1, row, :])
                ce = jnp.where(last_row, edge_e, pltpu.roll(c, LON - 1, 0))
                cw = jnp.where(first_row, edge_w, pltpu.roll(c, 1, 0))
                cn = pltpu.roll(c, LAT - 1, 1)
                vert = kl * (x[t, n + 1] - c) - kb * (c - x[t, n - 1])
                if adjoint:
                    cs = pltpu.roll(c, 1, 1)
                    y = c + (a * (ce - c) + bw * (c - cw)) + (p * (cn - c) + qs * (c - cs)) + vert
                else:
                    fn = p * c + q * cn
                    y = c - (a * c + b * ce) + (aw * cw + bw * c) - fn + pltpu.roll(fn, 1, 1) + vert
                put(t, n, y)

        loop(low, high, one)

    def put_in(x):
        def put(t, n, y):
            x[t, n] = y

        return put

    lev_copies[0].wait_recv()

    @pl.when(lev == 0)
    def _():
        k[0:2] = jnp.zeros((2, LON, LAT), F32)

    finish_lon(0)
    edge_u[...] = lon_in[0, 0, 24:32]

    @pl.when(tile == 0)
    def _():
        edge_u[...] = jnp.zeros((8, LAT), F32)

    sweep(x0, 0, False, 2, 8, put_in(x1))
    for t in range(TR):
        x1[t, 1] = k[1] * x0[t, 2]
        x1[t, 8] = k[7] * x0[t, 7]

    @pl.when(lev == NLEV - 1)
    def _():
        x1[:, 8] = blank

    stage_lon(x1, 1, 1, 9)
    loop(2, 8, stage_winds)
    lon_out[1, 0, 40] = k[1, LON - 1]
    lon_out[1, 1, 40] = k[1, 0]
    lons.append(lon_copies(1))
    for copy in lons[1]:
        copy.start()

    loop(1, NTILE, ids_wait)

    def unpack(c):
        left, right = [], []
        for h in range(2):
            a, b = ids_in[c * 4 + h * 2], ids_in[c * 4 + h * 2 + 1]
            left.append(jnp.where(half, a, pltpu.roll(b, CAP, 1)))
            right.append(jnp.where(half, pltpu.roll(a, CAP, 1), b))
        ga, gb = jnp.concatenate(left, axis=1), jnp.concatenate(right, axis=1)
        fb[c] = gb
        ga = ga.astype(I32)
        kindhot[c] = onehot(KIND, gb[0:1, :].astype(I32))
        for j in range(FOOT):
            cols = slice(j * CHUNK, (j + 1) * CHUNK)
            lat = onehot(LAT, ga[j : j + 1, :]).astype(BF16)
            lathot[c, 0:LAT, cols] = lat
            lathot[c, LAT : 2 * LAT, cols] = lat
            lon = onehot(LON, ga[4 + j : 5 + j, :])
            lonhot[c, :, cols] = lon
            lonbits[c, :, cols] = lon.astype(BF16)

    loop(0, NLEV, unpack)

    for copy in lev_copies[1:] + diag_copies:
        copy.wait_recv()
    edge_u[0:1] = diag_in[0, 6:7]
    edge_u[7:8] = diag_in[1, 1:2]

    @pl.when(tile == 0)
    def _():
        edge_u[...] = jnp.zeros((8, LAT), F32)

    @pl.when(lev == 0)
    def _():
        kern_all[1] = jnp.zeros((KIND, 128), F32)

    @pl.when(lev == NLEV - 1)
    def _():
        kern_all[2] = jnp.zeros((KIND, 128), F32)

    for n in range(EXT):
        which, col = (1, 4 + n) if n < 2 else (0, n - 2) if n < 8 else (2, n - 8)
        kern_wide[n] = jnp.broadcast_to(kern_all[which, :, col : col + 1], (KIND, 128))

    finish_lon(1)
    sweep(x1, 1, False, 1, 9, put_in(x2))
    for t in range(TR):
        x2[t, 0] = k[0] * x1[t, 1]
        x2[t, 9] = k[8] * x1[t, 8]

    def profile(i):
        t, h = i // 2, lax.rem(i, 2)
        rows = pl.ds(pl.multiple_of(h * 16, 16), 16)
        for w in range(LAT // 128):
            cols = slice(w * 128, (w + 1) * 128)
            planes = [x2[t, n, rows, cols] for n in range(EXT)]
            for j in range(KIND):
                acc = planes[0] * kern_wide[0, j : j + 1, :]
                for n in range(1, EXT):
                    acc = acc + planes[n] * kern_wide[n, j : j + 1, :]
                high, low = parts_of(acc, 2)
                to = pl.ds(pl.multiple_of(t * PER + j * LON + h * 16, 16), 16)
                e[to, cols] = high
                e[to, LAT + w * 128 : LAT + (w + 1) * 128] = low

    loop(0, 2 * TR, profile)

    def part_copy(c, d):
        peer = lax.rem(lev + d, NLEV)
        return remote(part_out.at[c], part_in.at[lev, c], part_ss.at[c, d], part_rs.at[c, d], {"lev": peer})

    def part_wait(c, d):
        source = lax.rem(lev + NLEV - d, NLEV)
        remote(
            part_out.at[c], part_in.at[source, c], part_ss.at[c, d], part_rs.at[c, d], {"lev": source}
        ).wait_recv()

    def gather(c):
        picked[...] = jnp.dot(e[...], lathot[c], preferred_element_type=F32)
        mask = lonhot[c]
        for t in range(TR):
            acc = jnp.zeros((LON, CHUNK), F32)
            for j in range(KIND):
                r = t * PER + j * LON
                block = picked[r : r + LON, :] * mask
                block = (block[:, 0:CHUNK] + block[:, CHUNK : 2 * CHUNK]) + (
                    block[:, 2 * CHUNK : 3 * CHUNK] + block[:, 3 * CHUNK :]
                )
                acc = acc + block * kindhot[c, j : j + 1, :]
            row = jnp.sum(acc, axis=0, keepdims=True)
            part_out[c, t : t + 1, :] = row[:, 0:128]
            part_out[c, 3 + t : 4 + t, :] = row[:, 128:256]
        part_in[lev, c] = part_out[c]
        for d in range(1, NLEV):
            part_copy(c, d).start()

    loop(0, NLEV, gather)

    def ret_copy(peer):
        d = lax.rem(peer + NTILE - tile, NTILE)
        return remote(res.at[peer // 4], ret_in.at[tile], ret_ss.at[d], ret_rs.at[d], {"tile": peer})

    def ret_wait(d):
        source = lax.rem(tile + NTILE - d, NTILE)
        remote(res.at[source // 4], ret_in.at[source], ret_ss.at[d], ret_rs.at[d], {"tile": source}).wait_recv()

    total[...] = jnp.zeros((ROWS, LAT), F32)

    def scatter(c):
        for d in range(1, NLEV):
            part_wait(c, d)
        model = part_in[0, c]
        for z in range(1, NLEV):
            model = model + part_in[z, c]
        seen = jnp.concatenate([fb[c, 1:4, 0:128], fb[c, 1:4, 128:256]], axis=0)
        res[c, 0:6] = model[0:6] * (1.0 / FOOT) - seen
        for n in range(4):
            peer = c * 4 + n

            @pl.when(peer != tile)
            def _():
                ret_copy(peer).start()

        mask = lonbits[c]
        for t in range(TR):
            row = jnp.concatenate([res[c, t : t + 1, :], res[c, 3 + t : 4 + t, :]], axis=1)
            row = row * fb[c, 4:5, :] * (1.0 / FOOT)
            for h, piece in enumerate(parts_of(row, 2)):
                piece = piece.astype(F32)
                for j in range(KIND):
                    value = jnp.broadcast_to(piece * kindhot[c, j : j + 1, :], (16, CHUNK)).astype(BF16)
                    value = jnp.concatenate([value] * FOOT, axis=1)
                    r = h * PER + j * LON
                    terms[t, r : r + 16, :] = mask[0:16] * value
                    terms[t, r + 16 : r + 32, :] = mask[16:32] * value
            got = lax.dot_general(terms[t], lathot[c, 0:LAT, :], NT, preferred_element_type=F32)
            total[t * PER : (t + 1) * PER, :] += got[0:PER] + got[PER:]

    loop(0, NLEV, scatter)
    ret_in[tile] = res[tile // 4]

    def force(i):
        t, h = i // 4, lax.rem(i, 4)
        rows = pl.ds(pl.multiple_of(h * 8, 8), 8)
        for w in range(LAT // 128):
            cols = slice(w * 128, (w + 1) * 128)
            sums = [
                total[pl.ds(pl.multiple_of(t * PER + j * LON + h * 8, 8), 8), cols] for j in range(KIND)
            ]
            for n in range(EXT):
                acc = sums[0] * kern_wide[n, 0:1, :]
                for j in range(1, KIND):
                    acc = acc + sums[j] * kern_wide[n, j : j + 1, :]
                x2[t, n, rows, cols] = acc

    loop(0, 4 * TR, force)
    stage_lon(x2, 2, 1, 9)
    lons.append(lon_copies(2))
    for copy in lons[2]:
        copy.start()

    loop(1, NTILE, ret_wait)
    pair_odd, odd = lax.rem(tile // 2, 2) == 1, lax.rem(tile, 2) == 1
    keep = lax.broadcasted_iota(I32, (8, 128), 0) < TR

    def regroup(i):
        halves = []
        for h in range(2):
            got = ret_in[2 * i + h]
            got = jnp.where(pair_odd, pltpu.roll(got, 5, 0), got)
            moved = pltpu.roll(got, CAP, 1)
            halves.append(jnp.where(odd, got, moved) if h else jnp.where(odd, moved, got))
        both = jnp.where(half, halves[0], halves[1])
        cols = pl.ds(pl.multiple_of(i * 128, 128), 128)
        for j, piece in enumerate(parts_of(jnp.where(keep, both, 0.0), 3)):
            spread[j * 8 : j * 8 + 8, cols] = piece.astype(F32)

    loop(0, NTILE // 2, regroup)
    back = jnp.concatenate([spread[...], jnp.zeros((8, SLOTS), F32)], axis=0).astype(BF16)
    back = jnp.dot(back, hot[...], preferred_element_type=F32)
    residual[...] = (back[0:8] + back[8:16] + back[16:24])[0:TR]

    finish_lon(2)
    sweep(x2, 2, True, 1, 9, put_in(x3))

    @pl.when(lev == NLEV - 1)
    def _():
        x3[:, 8] = blank

    lane = lax.broadcasted_iota(I32, (8, LAT), 1) < LAT - 1
    here_u = edge_u[...]
    east_u = jnp.concatenate([u[n, LON - 1 : LON, :] for n in range(8)], axis=0)
    for side in range(2):
        wind = lon_in[1, side, 24:32, :]
        right, left = (here_u, wind) if side == 0 else (wind, east_u)
        north = jnp.where(lane, lon_in[1, side, 32:40, :], 0.0)
        up_k = lon_in[1, side, 40:48, :]
        low_k = pltpu.roll(up_k, 1, 0)
        a, bw = jnp.maximum(right, 0.0), jnp.minimum(left, 0.0)
        p, qs = jnp.maximum(north, 0.0), pltpu.roll(jnp.minimum(north, 0.0), 1, 1)
        for t in range(TR):
            c = lon_in[2, side, t * 8 : t * 8 + 8, :]
            far = lon_in[2, side, 24 + t * 8 : 32 + t * 8, :]
            near = jnp.concatenate([x2[t, n, side * (LON - 1) : side * (LON - 1) + 1, :] for n in range(1, 9)], axis=0)
            ce, cw = (near, far) if side == 0 else (far, near)
            cn, cs = pltpu.roll(c, LAT - 1, 1), pltpu.roll(c, 1, 1)
            vert = up_k * (pltpu.roll(c, 7, 0) - c) - low_k * (c - pltpu.roll(c, 1, 0))
            edge_y[side, t * 8 : t * 8 + 8, :] = (
                c + (a * (ce - c) + bw * (c - cw)) + (p * (cn - c) + qs * (c - cs)) + vert
            )

    @pl.when(tile == NTILE - 1)
    def _():
        edge_y[1] = jnp.zeros((24, LAT), F32)

    def put_gradient(t, n, y):
        gradient[t, n - 2] = y

    sweep(x3, 3, True, 2, 8, put_gradient)

    for copies in lons + [lev_copies, diag_copies]:
        for copy in copies:
            copy.wait_send()
    loop(1, NTILE, lambda d: ids_copy(d).wait_send())
    loop(1, NTILE, lambda d: ret_copy(lax.rem(tile + d, NTILE)).wait_send())

    def parts_sent(c):
        for d in range(1, NLEV):
            part_copy(c, d).wait_send()

    loop(0, NLEV, parts_sent)


def store(a, b, a_out, b_out, a_held, b_held, in_sem, out_sem):
    into = [pltpu.make_async_copy(b.at[t], b_held.at[t], in_sem.at[t]) for t in range(TR)]
    out = [pltpu.make_async_copy(b_held.at[t], b_out.at[t], out_sem.at[t]) for t in range(TR)]
    into.append(pltpu.make_async_copy(a, a_held, in_sem.at[TR]))
    out.append(pltpu.make_async_copy(a_held, a_out, out_sem.at[TR]))
    for copy in into:
        copy.start()
    for got, put in zip(into, out):
        got.wait()
        put.start()
    for copy in out:
        copy.wait()


def body(conc, u_wind, v_wind, mixing, kernels, observed, obs_weight, column_tile, footprint, kernel_index):
    dma = pltpu.SemaphoreType.DMA
    hbm, vmem = pl.BlockSpec(memory_space=pl.ANY), pl.BlockSpec(memory_space=pltpu.VMEM)
    ext = pltpu.VMEM((TR, EXT, LON, LAT), F32)
    shapes = (
        jax.ShapeDtypeStruct((TR, SND), F32),
        jax.ShapeDtypeStruct((TR, LV, LON, LAT), F32),
    )
    found = pl.pallas_call(
        kernel,
        out_shape=shapes,
        in_specs=[hbm] * 10,
        out_specs=(vmem, vmem),
        scratch_shapes=[
            pltpu.VMEM((KIND, LV), F32),
            pltpu.VMEM((TR, SND), F32),
            pltpu.VMEM((1, SND), F32),
            pltpu.VMEM((1, SND), I32),
            pltpu.VMEM((FOOT, SND), I32),
            pltpu.VMEM((1, SND), I32),
            ext, ext, ext, ext,
            pltpu.VMEM((LV + 2, LON, LAT), F32),
            pltpu.VMEM((LV + 2, LON, LAT), F32),
            pltpu.VMEM((LV + 3, LON, LAT), F32),
            pltpu.VMEM((3, 2, 48, LAT), F32),
            pltpu.VMEM((3, 2, 48, LAT), F32),
            pltpu.VMEM((8, LAT), F32),
            pltpu.VMEM((2, 8, LAT), F32),
            pltpu.VMEM((2, 24, LAT), F32),
            pltpu.VMEM((3, KIND, 128), F32),
            pltpu.VMEM((EXT, KIND, 128), F32),
            pltpu.VMEM((16, SND), F32),
            pltpu.VMEM((NTILE, 8, 128), F32),
            pltpu.VMEM((NTILE, 8, 128), F32),
            pltpu.VMEM((SLOTS, SND), BF16),
            pltpu.VMEM((NLEV, 8, CHUNK), F32),
            pltpu.VMEM((NLEV, KIND, CHUNK), F32),
            pltpu.VMEM((NLEV, 2 * LAT, LOOK), BF16),
            pltpu.VMEM((NLEV, LON, LOOK), F32),
            pltpu.VMEM((NLEV, LON, LOOK), BF16),
            pltpu.VMEM((24, SLOTS), F32),
            pltpu.VMEM((ROWS, 2 * LAT), BF16),
            pltpu.VMEM((ROWS, LOOK), F32),
            pltpu.VMEM((NLEV, 8, 128), F32),
            pltpu.VMEM((NLEV, NLEV, 8, 128), F32),
            pltpu.VMEM((NLEV, 8, 128), F32),
            pltpu.VMEM((NTILE, 8, 128), F32),
            pltpu.VMEM((TR, 2 * PER, LOOK), BF16),
            pltpu.VMEM((ROWS, LAT), F32),
            dma((10,)),
            dma((8,)), dma((8,)),
            dma((2,)), dma((2,)),
            dma((3, 2)), dma((3, 2)),
            dma((NTILE,)), dma((NTILE,)),
            dma((NLEV, NLEV)), dma((NLEV, NLEV)),
            dma((NTILE,)), dma((NTILE,)),
        ],
        compiler_params=pltpu.CompilerParams(
            collective_id=0, has_side_effects=True, vmem_limit_bytes=60 * 1024 * 1024
        ),
    )(
        conc, u_wind, v_wind, mixing, kernels, observed, obs_weight[None], column_tile.T, footprint.T, kernel_index[None]
    )
    return pl.pallas_call(
        store,
        out_shape=shapes,
        in_specs=[hbm] * 2,
        out_specs=(hbm, hbm),
        scratch_shapes=[
            pltpu.VMEM((TR, SND), F32),
            pltpu.VMEM((TR, LV, LON, LAT), F32),
            dma((TR + 1,)),
            dma((TR + 1,)),
        ],
        compiler_params=pltpu.CompilerParams(vmem_limit_bytes=60 * 1024 * 1024),
    )(*found)


def solution(mesh):
    placed = (
        P(None, "lev", "tile", None),
        P("lev", "tile", None),
        P("lev", "tile", None),
        P("lev", "tile", None),
        P(None, "lev"),
        P(None, "tile"),
        P("tile"),
        P("tile", None),
        P("tile", None),
        P("tile"),
    )
    return jax.shard_map(
        body,
        mesh=mesh,
        in_specs=placed,
        out_specs=(P(None, "tile"), P(None, "lev", "tile", None)),
        check_vma=False,
    )
```

```python
import jax
import jax.numpy as jnp
from jax import lax
from jax.experimental import pallas as pl
from jax.experimental.pallas import tpu as pltpu
from jax.sharding import PartitionSpec as P

MESH = pl.DeviceIdType.MESH
F32, BF16, I32 = jnp.float32, jnp.bfloat16, jnp.int32
NT = (((1,), (1,)), ((), ()))
TR, LV, LON, LAT, KIND = 3, 6, 32, 384, 8
EXT = LV + 4
ROWS = TR * KIND * LON
PER = KIND * LON
NTILE, NLEV, CAP, SND, FOOT = 32, 8, 64, 1024, 4
SLOTS = NTILE * CAP
CHUNK = SLOTS // NLEV
LOOK = FOOT * CHUNK


def parts_of(x, count):
    pieces = []
    for _ in range(count):
        piece = x.astype(BF16)
        pieces.append(piece)
        x = x - piece.astype(F32)
    return pieces


def onehot(rows, index, base=0):
    shape = (rows, index.shape[1])
    return (lax.broadcasted_iota(I32, shape, 0) + base == index).astype(F32)


def unrolled(low, high, body):
    for i in range(low, high):
        body(i)


def loop(low, high, body):
    def step(i, carry):
        body(i)
        return carry

    lax.fori_loop(low, high, step, 0)


def kernel(
    conc, u_in, v_in, k_in, kern_in, observed_in, weight_in, column_in, feet_in, kinds_in,
    residual, gradient,
    kern, observed, weight, column, feet, kinds, x0, x1, x2, x3, u, v, k, lon_out, lon_in, edge_u, diag_in, edge_y, kern_all, kern_wide, fields,
    ids_out, ids_in, hot, fb, kindhot, code, lathot, lonhot, cellhot, spread,
    e, picked, part_out, part_in, res, ret_in, terms, total,
    local_sem, lev_ss, lev_rs, diag_ss, diag_rs, lon_ss, lon_rs, ids_ss, ids_rs, part_ss, part_rs, ret_ss, ret_rs,
):
    tile, lev = lax.axis_index("tile"), lax.axis_index("lev")
    east, west = lax.rem(tile + 1, NTILE), lax.rem(tile + NTILE - 1, NTILE)
    above, below = lax.rem(lev + 1, NLEV), lax.rem(lev + NLEV - 1, NLEV)

    def remote(src, dst, ss, rs, target):
        return pltpu.make_async_remote_copy(
            src_ref=src, dst_ref=dst, send_sem=ss, recv_sem=rs, device_id=target, device_id_type=MESH
        )

    barrier = pltpu.get_barrier_semaphore()

    def greet(target):
        pl.semaphore_signal(barrier, inc=1, device_id=target, device_id_type=MESH)

    loop(1, NLEV, lambda d: greet({"lev": lax.rem(lev + d, NLEV)}))
    loop(1, NTILE, lambda d: greet({"tile": lax.rem(tile + d, NTILE)}))
    greet({"tile": west, "lev": below})
    greet({"tile": west, "lev": above})
    own = pl.ds(2, LV)
    loads = [
        pltpu.make_async_copy(conc, x0.at[:, own], local_sem.at[0]),
        pltpu.make_async_copy(u_in, u.at[pl.ds(1, LV)], local_sem.at[1]),
        pltpu.make_async_copy(v_in, v.at[pl.ds(1, LV)], local_sem.at[2]),
        pltpu.make_async_copy(k_in, k.at[own], local_sem.at[3]),
    ]
    small = [(kern_in, kern), (observed_in, observed), (weight_in, weight), (column_in, column), (feet_in, feet), (kinds_in, kinds)]
    smalls = [pltpu.make_async_copy(src, dst, local_sem.at[4 + n]) for n, (src, dst) in enumerate(small)]
    for copy in smalls + loads:
        copy.start()
    for copy in smalls:
        copy.wait()

    half = lax.broadcasted_iota(I32, (8, 128), 1) < CAP

    foot = feet[...]
    foot_lon = lax.shift_right_logical(lax.shift_right_logical(foot, 7) * 171, 9)
    fields[0:4, :] = (foot - foot_lon * LAT).astype(F32)
    fields[4:8, :] = foot_lon.astype(F32)
    fields[8:9, :] = kinds[...].astype(F32)
    fields[9:12, :] = observed[...]
    fields[12:13, :] = weight[...]
    fields[13:16, :] = jnp.zeros((3, SND), F32)
    target = column[...]
    match = onehot(NTILE, target)
    earlier = (
        lax.broadcasted_iota(I32, (SND, SND), 0) < lax.broadcasted_iota(I32, (SND, SND), 1)
    ).astype(F32).astype(BF16)
    before = jnp.dot(match.astype(BF16), earlier, preferred_element_type=F32)
    slot = target * CAP + jnp.sum(before * match, axis=0, keepdims=True).astype(I32)
    data = jnp.concatenate([p.astype(F32) for p in parts_of(fields[...], 3)], axis=0).astype(BF16)

    def pack(i):
        rows = pl.ds(pl.multiple_of(i * CHUNK, CHUNK), CHUNK)
        hot[rows, :] = onehot(CHUNK, slot, i * CHUNK).astype(BF16)
        got = lax.dot_general(data, hot[rows, :], NT, preferred_element_type=F32)
        got = got[0:16] + got[16:32] + got[32:48]
        for h in range(2):
            a, b = got[0:8, h * 128 : h * 128 + 128], got[8:16, h * 128 : h * 128 + 128]
            ids_out[i * 4 + h * 2] = jnp.where(half, a, pltpu.roll(b, CAP, 1))
            ids_out[i * 4 + h * 2 + 1] = jnp.where(half, pltpu.roll(a, CAP, 1), b)

    loop(0, NLEV, pack)
    ids_in[tile] = ids_out[tile]
    kern_all[0, :, 0:LV] = kern[...]

    blank = jnp.zeros((TR, LON, LAT), F32)
    x0[:, 1], x0[:, 8] = blank, blank
    x1[:, 0], x1[:, 9] = blank, blank

    def lon_copies(i):
        rows = pl.ds(0, 48 if i else 32)
        return [
            remote(
                lon_out.at[i, side, rows], lon_in.at[i, side, rows], lon_ss.at[i, side], lon_rs.at[i, side], {"tile": to}
            )
            for side, to in enumerate((east, west))
        ]

    def stage_lon(x, i, low, high):
        def one(n):
            for t in range(TR):
                lon_out[i, 0, t * 8 + n - 1] = x[t, n, LON - 1]
                lon_out[i, 1, t * 8 + n - 1] = x[t, n, 0]
                if i == 2:
                    lon_out[i, 0, 23 + t * 8 + n] = x[t, n, LON - 2]
                    lon_out[i, 1, 23 + t * 8 + n] = x[t, n, 1]
            if i == 0:
                lon_out[i, 0, 23 + n] = u[n - 1, LON - 1]

        unrolled(low, high, one)

    def stage_winds(n):
        lon_out[1, 0, 23 + n] = u[n - 1, LON - 2]
        lon_out[1, 1, 23 + n] = u[n - 1, 0]
        lon_out[1, 0, 31 + n] = v[n - 1, LON - 1]
        lon_out[1, 1, 31 + n] = v[n - 1, 0]
        lon_out[1, 0, 39 + n] = k[n, LON - 1]
        lon_out[1, 1, 39 + n] = k[n, 0]

    def finish_lon(i):
        for copy in lons[i]:
            copy.wait_recv()

        @pl.when(tile == NTILE - 1)
        def _():
            lon_in[i, 1] = jnp.zeros((48, LAT), F32)

    for copy in loads:
        copy.wait()
    stage_lon(x0, 0, 2, 8)

    lev_moves = [
        (k.at[pl.ds(LV, 2)], k.at[pl.ds(0, 2)], above),
        (kern_all.at[0], kern_all.at[1], above),
        (kern_all.at[0], kern_all.at[2], below),
        (u.at[LV], u.at[0], above),
        (u.at[1], u.at[LV + 1], below),
        (v.at[LV], v.at[0], above),
        (v.at[1], v.at[LV + 1], below),
        (k.at[2], k.at[LV + 2], below),
    ]
    lev_copies = [
        remote(src, dst, lev_ss.at[n], lev_rs.at[n], {"lev": to}) for n, (src, dst, to) in enumerate(lev_moves)
    ]
    lons = [lon_copies(0)]
    diag_copies = [
        remote(
            lon_out.at[0, 0, pl.ds(24, 8)], diag_in.at[n], diag_ss.at[n], diag_rs.at[n], {"tile": east, "lev": to}
        )
        for n, to in enumerate((above, below))
    ]

    def ids_copy(d):
        peer = lax.rem(tile + d, NTILE)
        return remote(ids_out.at[peer], ids_in.at[tile], ids_ss.at[d], ids_rs.at[d], {"tile": peer})

    def ids_wait(source):
        d = lax.rem(tile + NTILE - source, NTILE)
        remote(ids_out.at[source], ids_in.at[source], ids_ss.at[d], ids_rs.at[d], {"tile": source}).wait_recv()

    pl.semaphore_wait(barrier, NTILE - 1 + NLEV - 1 + 2)
    for copy in lons[0] + lev_copies[0:1]:
        copy.start()
    loop(1, NTILE, lambda d: ids_copy(d).start())
    for copy in diag_copies + lev_copies[1:]:
        copy.start()

    last_row = lax.broadcasted_iota(I32, (LON, LAT), 0) == LON - 1
    first_row = lax.broadcasted_iota(I32, (LON, LAT), 0) == 0
    open_face = lax.broadcasted_iota(I32, (LON, LAT), 1) < LAT - 1

    def sweep(x, i, adjoint, low, high, put):
        def one(n):
            ul, kl, kb = u[n - 1], k[n], k[n - 1]
            uw = jnp.where(first_row, edge_u[pl.ds(n - 1, 1), :], pltpu.roll(ul, 1, 0))
            vl = jnp.where(open_face, v[n - 1], 0.0)
            a, bw = jnp.maximum(ul, 0.0), jnp.minimum(uw, 0.0)
            p, q = jnp.maximum(vl, 0.0), jnp.minimum(vl, 0.0)
            if adjoint:
                qs = pltpu.roll(q, 1, 1)
            else:
                b, aw = jnp.minimum(ul, 0.0), jnp.maximum(uw, 0.0)
            for t in range(TR):
                row = pl.ds(t * 8 + n - 1, 1)
                c = x[t, n]
                edge_w, edge_e = (lon_in[i, 0, row, :], lon_in[i, 1, row, :]) if i < 3 else (edge_y[0, row, :], edge_y[1, row, :])
                ce = jnp.where(last_row, edge_e, pltpu.roll(c, LON - 1, 0))
                cw = jnp.where(first_row, edge_w, pltpu.roll(c, 1, 0))
                cn = pltpu.roll(c, LAT - 1, 1)
                vert = kl * (x[t, n + 1] - c) - kb * (c - x[t, n - 1])
                if adjoint:
                    cs = pltpu.roll(c, 1, 1)
                    y = c + (a * (ce - c) + bw * (c - cw)) + (p * (cn - c) + qs * (c - cs)) + vert
                else:
                    fn = p * c + q * cn
                    y = c - (a * c + b * ce) + (aw * cw + bw * c) - fn + pltpu.roll(fn, 1, 1) + vert
                put(t, n, y)

        loop(low, high, one)

    def put_in(x):
        def put(t, n, y):
            x[t, n] = y

        return put

    lev_copies[0].wait_recv()

    @pl.when(lev == 0)
    def _():
        k[0:2] = jnp.zeros((2, LON, LAT), F32)

    finish_lon(0)
    edge_u[...] = lon_in[0, 0, 24:32]

    @pl.when(tile == 0)
    def _():
        edge_u[...] = jnp.zeros((8, LAT), F32)

    sweep(x0, 0, False, 2, 8, put_in(x1))
    for t in range(TR):
        x1[t, 1] = k[1] * x0[t, 2]
        x1[t, 8] = k[7] * x0[t, 7]

    @pl.when(lev == NLEV - 1)
    def _():
        x1[:, 8] = blank

    stage_lon(x1, 1, 1, 9)
    loop(2, 8, stage_winds)
    lon_out[1, 0, 40] = k[1, LON - 1]
    lon_out[1, 1, 40] = k[1, 0]
    lons.append(lon_copies(1))
    for copy in lons[1]:
        copy.start()

    def unpack(i):
        c = lax.rem(tile // 4 + i, NLEV)
        for n in range(4):
            source = c * 4 + n

            @pl.when(source != tile)
            def _():
                ids_wait(source)

        left, right = [], []
        for h in range(2):
            a, b = ids_in[c * 4 + h * 2], ids_in[c * 4 + h * 2 + 1]
            left.append(jnp.where(half, a, pltpu.roll(b, CAP, 1)))
            right.append(jnp.where(half, pltpu.roll(a, CAP, 1), b))
        ga, gb = jnp.concatenate(left, axis=1), jnp.concatenate(right, axis=1)
        fb[c] = gb
        ga = ga.astype(I32)
        kind = gb[0:1, :].astype(I32)
        kindhot[c] = onehot(KIND, kind)
        code[c] = kind * LON + ga[4:8, :]
        for j in range(FOOT):
            cols = slice(j * CHUNK, (j + 1) * CHUNK)
            lat = onehot(LAT, ga[j : j + 1, :]).astype(BF16)
            lathot[c, 0:LAT, cols] = lat
            lathot[c, LAT : 2 * LAT, cols] = lat
            lonhot[c, :, cols] = onehot(LON, ga[4 + j : 5 + j, :])

    loop(0, NLEV, unpack)

    for copy in lev_copies[1:] + diag_copies:
        copy.wait_recv()
    edge_u[0:1] = diag_in[0, 6:7]
    edge_u[7:8] = diag_in[1, 1:2]

    @pl.when(tile == 0)
    def _():
        edge_u[...] = jnp.zeros((8, LAT), F32)

    @pl.when(lev == 0)
    def _():
        kern_all[1] = jnp.zeros((KIND, 128), F32)

    @pl.when(lev == NLEV - 1)
    def _():
        kern_all[2] = jnp.zeros((KIND, 128), F32)

    for n in range(EXT):
        which, col = (1, 4 + n) if n < 2 else (0, n - 2) if n < 8 else (2, n - 8)
        kern_wide[n] = jnp.broadcast_to(kern_all[which, :, col : col + 1], (KIND, 128))

    finish_lon(1)
    sweep(x1, 1, False, 1, 9, put_in(x2))
    for t in range(TR):
        x2[t, 0] = k[0] * x1[t, 1]
        x2[t, 9] = k[8] * x1[t, 8]

    def profile(i):
        t, h = i // 2, lax.rem(i, 2)
        rows = pl.ds(pl.multiple_of(h * 16, 16), 16)
        for w in range(LAT // 128):
            cols = slice(w * 128, (w + 1) * 128)
            planes = [x2[t, n, rows, cols] for n in range(EXT)]
            for j in range(KIND):
                acc = planes[0] * kern_wide[0, j : j + 1, :]
                for n in range(1, EXT):
                    acc = acc + planes[n] * kern_wide[n, j : j + 1, :]
                high, low = parts_of(acc, 2)
                to = pl.ds(pl.multiple_of(t * PER + j * LON + h * 16, 16), 16)
                e[to, cols] = high
                e[to, LAT + w * 128 : LAT + (w + 1) * 128] = low

    loop(0, 2 * TR, profile)

    def part_copy(c, d):
        peer = lax.rem(lev + d, NLEV)
        return remote(part_out.at[c], part_in.at[lev, c], part_ss.at[c, d], part_rs.at[c, d], {"lev": peer})

    def part_wait(c, d):
        source = lax.rem(lev + NLEV - d, NLEV)
        remote(
            part_out.at[c], part_in.at[source, c], part_ss.at[c, d], part_rs.at[c, d], {"lev": source}
        ).wait_recv()

    def gather(c):
        picked[...] = jnp.dot(e[...], lathot[c], preferred_element_type=F32)
        for j in range(FOOT):
            cellhot[c, :, j * CHUNK : (j + 1) * CHUNK] = onehot(PER, code[c, j : j + 1, :]).astype(BF16)
        mask = lonhot[c]
        for t in range(TR):
            acc = jnp.zeros((LON, CHUNK), F32)
            for j in range(KIND):
                r = t * PER + j * LON
                block = picked[r : r + LON, :] * mask
                block = (block[:, 0:CHUNK] + block[:, CHUNK : 2 * CHUNK]) + (
                    block[:, 2 * CHUNK : 3 * CHUNK] + block[:, 3 * CHUNK :]
                )
                acc = acc + block * kindhot[c, j : j + 1, :]
            row = jnp.sum(acc, axis=0, keepdims=True)
            part_out[c, t : t + 1, :] = row[:, 0:128]
            part_out[c, 3 + t : 4 + t, :] = row[:, 128:256]
        part_in[lev, c] = part_out[c]
        for d in range(1, NLEV):
            part_copy(c, d).start()

    loop(0, NLEV, gather)

    def ret_copy(peer):
        d = lax.rem(peer + NTILE - tile, NTILE)
        return remote(res.at[peer // 4], ret_in.at[tile], ret_ss.at[d], ret_rs.at[d], {"tile": peer})

    def ret_wait(d):
        source = lax.rem(tile + NTILE - d, NTILE)
        remote(res.at[source // 4], ret_in.at[source], ret_ss.at[d], ret_rs.at[d], {"tile": source}).wait_recv()

    total[...] = jnp.zeros((PER, 2 * TR * LAT), F32)

    def settle(c):
        for d in range(1, NLEV):
            part_wait(c, d)
        model = part_in[0, c]
        for z in range(1, NLEV):
            model = model + part_in[z, c]
        seen = jnp.concatenate([fb[c, 1:4, 0:128], fb[c, 1:4, 128:256]], axis=0)
        res[c, 0:6] = model[0:6] * (1.0 / FOOT) - seen
        for n in range(4):
            peer = c * 4 + n

            @pl.when(peer != tile)
            def _():
                ret_copy(peer).start()

    ahead = 3
    loop(0, ahead, settle)

    def scatter(c):
        @pl.when(c < NLEV - ahead)
        def _():
            settle(c + ahead)

        for t in range(TR):
            row = jnp.concatenate([res[c, t : t + 1, :], res[c, 3 + t : 4 + t, :]], axis=1)
            row = row * fb[c, 4:5, :] * (1.0 / FOOT)
            for h, piece in enumerate(parts_of(row, 2)):
                value = jnp.broadcast_to(piece.astype(F32), (16, CHUNK)).astype(BF16)
                value = jnp.concatenate([value] * FOOT, axis=1)
                for r in range(0, LAT, 16):
                    terms[t, h * LAT + r : h * LAT + r + 16, :] = lathot[c, r : r + 16, :] * value
            cols = slice(t * 2 * LAT, (t + 1) * 2 * LAT)
            total[:, cols] += lax.dot_general(cellhot[c], terms[t], NT, preferred_element_type=F32)

    loop(0, NLEV, scatter)
    ret_in[tile] = res[tile // 4]

    def force(h):
        rows = pl.ds(pl.multiple_of(h * 8, 8), 8)
        for t in range(TR):
            for w in range(LAT // 128):
                cols = slice(w * 128, (w + 1) * 128)
                start_high = t * 2 * LAT + w * 128
                high, low = slice(start_high, start_high + 128), slice(start_high + LAT, start_high + LAT + 128)
                sums = []
                for j in range(KIND):
                    cells = pl.ds(pl.multiple_of(j * LON + h * 8, 8), 8)
                    sums.append(total[cells, high] + total[cells, low])
                for n in range(EXT):
                    acc = sums[0] * kern_wide[n, 0:1, :]
                    for j in range(1, KIND):
                        acc = acc + sums[j] * kern_wide[n, j : j + 1, :]
                    x2[t, n, rows, cols] = acc

    loop(0, 2, lambda i: force(i * 3))
    stage_lon(x2, 2, 1, 9)
    lons.append(lon_copies(2))
    for copy in lons[2]:
        copy.start()
    loop(1, 3, force)

    loop(1, NTILE, ret_wait)
    pair_odd, odd = lax.rem(tile // 2, 2) == 1, lax.rem(tile, 2) == 1
    keep = lax.broadcasted_iota(I32, (8, 128), 0) < TR

    def regroup(i):
        halves = []
        for h in range(2):
            got = ret_in[2 * i + h]
            got = jnp.where(pair_odd, pltpu.roll(got, 5, 0), got)
            moved = pltpu.roll(got, CAP, 1)
            halves.append(jnp.where(odd, got, moved) if h else jnp.where(odd, moved, got))
        both = jnp.where(half, halves[0], halves[1])
        cols = pl.ds(pl.multiple_of(i * 128, 128), 128)
        for j, piece in enumerate(parts_of(jnp.where(keep, both, 0.0), 3)):
            spread[j * 8 : j * 8 + 8, cols] = piece.astype(F32)

    loop(0, NTILE // 2, regroup)
    back = jnp.concatenate([spread[...], jnp.zeros((8, SLOTS), F32)], axis=0).astype(BF16)
    back = jnp.dot(back, hot[...], preferred_element_type=F32)
    residual[...] = (back[0:8] + back[8:16] + back[16:24])[0:TR]

    finish_lon(2)
    sweep(x2, 2, True, 1, 9, put_in(x3))

    @pl.when(lev == NLEV - 1)
    def _():
        x3[:, 8] = blank

    lane = lax.broadcasted_iota(I32, (8, LAT), 1) < LAT - 1
    here_u = edge_u[...]
    east_u = jnp.concatenate([u[n, LON - 1 : LON, :] for n in range(8)], axis=0)
    for side in range(2):
        wind = lon_in[1, side, 24:32, :]
        right, left = (here_u, wind) if side == 0 else (wind, east_u)
        north = jnp.where(lane, lon_in[1, side, 32:40, :], 0.0)
        up_k = lon_in[1, side, 40:48, :]
        low_k = pltpu.roll(up_k, 1, 0)
        a, bw = jnp.maximum(right, 0.0), jnp.minimum(left, 0.0)
        p, qs = jnp.maximum(north, 0.0), pltpu.roll(jnp.minimum(north, 0.0), 1, 1)
        for t in range(TR):
            c = lon_in[2, side, t * 8 : t * 8 + 8, :]
            far = lon_in[2, side, 24 + t * 8 : 32 + t * 8, :]
            near = jnp.concatenate([x2[t, n, side * (LON - 1) : side * (LON - 1) + 1, :] for n in range(1, 9)], axis=0)
            ce, cw = (near, far) if side == 0 else (far, near)
            cn, cs = pltpu.roll(c, LAT - 1, 1), pltpu.roll(c, 1, 1)
            vert = up_k * (pltpu.roll(c, 7, 0) - c) - low_k * (c - pltpu.roll(c, 1, 0))
            edge_y[side, t * 8 : t * 8 + 8, :] = (
                c + (a * (ce - c) + bw * (c - cw)) + (p * (cn - c) + qs * (c - cs)) + vert
            )

    @pl.when(tile == NTILE - 1)
    def _():
        edge_y[1] = jnp.zeros((24, LAT), F32)

    def put_gradient(t, n, y):
        gradient[t, n - 2] = y

    sweep(x3, 3, True, 2, 8, put_gradient)

    for copies in lons + [lev_copies, diag_copies]:
        for copy in copies:
            copy.wait_send()
    unrolled(1, NTILE, lambda d: ids_copy(d).wait_send())
    unrolled(1, NTILE, lambda d: ret_copy(lax.rem(tile + d, NTILE)).wait_send())

    def parts_sent(c):
        for d in range(1, NLEV):
            part_copy(c, d).wait_send()

    loop(0, NLEV, parts_sent)


def store(a, b, a_out, b_out, a_held, b_held, in_sem, out_sem):
    into = [pltpu.make_async_copy(b.at[t], b_held.at[t], in_sem.at[t]) for t in range(TR)]
    out = [pltpu.make_async_copy(b_held.at[t], b_out.at[t], out_sem.at[t]) for t in range(TR)]
    into.append(pltpu.make_async_copy(a, a_held, in_sem.at[TR]))
    out.append(pltpu.make_async_copy(a_held, a_out, out_sem.at[TR]))
    for copy in into:
        copy.start()
    for got, put in zip(into, out):
        got.wait()
        put.start()
    for copy in out:
        copy.wait()


def body(conc, u_wind, v_wind, mixing, kernels, observed, obs_weight, column_tile, footprint, kernel_index):
    dma = pltpu.SemaphoreType.DMA
    hbm, vmem = pl.BlockSpec(memory_space=pl.ANY), pl.BlockSpec(memory_space=pltpu.VMEM)
    ext = pltpu.VMEM((TR, EXT, LON, LAT), F32)
    shapes = (
        jax.ShapeDtypeStruct((TR, SND), F32),
        jax.ShapeDtypeStruct((TR, LV, LON, LAT), F32),
    )
    found = pl.pallas_call(
        kernel,
        out_shape=shapes,
        in_specs=[hbm] * 10,
        out_specs=(vmem, vmem),
        scratch_shapes=[
            pltpu.VMEM((KIND, LV), F32),
            pltpu.VMEM((TR, SND), F32),
            pltpu.VMEM((1, SND), F32),
            pltpu.VMEM((1, SND), I32),
            pltpu.VMEM((FOOT, SND), I32),
            pltpu.VMEM((1, SND), I32),
            ext, ext, ext, ext,
            pltpu.VMEM((LV + 2, LON, LAT), F32),
            pltpu.VMEM((LV + 2, LON, LAT), F32),
            pltpu.VMEM((LV + 3, LON, LAT), F32),
            pltpu.VMEM((3, 2, 48, LAT), F32),
            pltpu.VMEM((3, 2, 48, LAT), F32),
            pltpu.VMEM((8, LAT), F32),
            pltpu.VMEM((2, 8, LAT), F32),
            pltpu.VMEM((2, 24, LAT), F32),
            pltpu.VMEM((3, KIND, 128), F32),
            pltpu.VMEM((EXT, KIND, 128), F32),
            pltpu.VMEM((16, SND), F32),
            pltpu.VMEM((NTILE, 8, 128), F32),
            pltpu.VMEM((NTILE, 8, 128), F32),
            pltpu.VMEM((SLOTS, SND), BF16),
            pltpu.VMEM((NLEV, 8, CHUNK), F32),
            pltpu.VMEM((NLEV, KIND, CHUNK), F32),
            pltpu.VMEM((NLEV, FOOT, CHUNK), I32),
            pltpu.VMEM((NLEV, 2 * LAT, LOOK), BF16),
            pltpu.VMEM((NLEV, LON, LOOK), F32),
            pltpu.VMEM((NLEV, PER, LOOK), BF16),
            pltpu.VMEM((24, SLOTS), F32),
            pltpu.VMEM((ROWS, 2 * LAT), BF16),
            pltpu.VMEM((ROWS, LOOK), F32),
            pltpu.VMEM((NLEV, 8, 128), F32),
            pltpu.VMEM((NLEV, NLEV, 8, 128), F32),
            pltpu.VMEM((NLEV, 8, 128), F32),
            pltpu.VMEM((NTILE, 8, 128), F32),
            pltpu.VMEM((TR, 2 * LAT, LOOK), BF16),
            pltpu.VMEM((PER, 2 * TR * LAT), F32),
            dma((10,)),
            dma((8,)), dma((8,)),
            dma((2,)), dma((2,)),
            dma((3, 2)), dma((3, 2)),
            dma((NTILE,)), dma((NTILE,)),
            dma((NLEV, NLEV)), dma((NLEV, NLEV)),
            dma((NTILE,)), dma((NTILE,)),
        ],
        compiler_params=pltpu.CompilerParams(
            collective_id=0, has_side_effects=True, vmem_limit_bytes=60 * 1024 * 1024
        ),
    )(
        conc, u_wind, v_wind, mixing, kernels, observed, obs_weight[None], column_tile.T, footprint.T, kernel_index[None]
    )
    return pl.pallas_call(
        store,
        out_shape=shapes,
        in_specs=[hbm] * 2,
        out_specs=(hbm, hbm),
        scratch_shapes=[
            pltpu.VMEM((TR, SND), F32),
            pltpu.VMEM((TR, LV, LON, LAT), F32),
            dma((TR + 1,)),
            dma((TR + 1,)),
        ],
        compiler_params=pltpu.CompilerParams(vmem_limit_bytes=60 * 1024 * 1024),
    )(*found)


def solution(mesh):
    placed = (
        P(None, "lev", "tile", None),
        P("lev", "tile", None),
        P("lev", "tile", None),
        P("lev", "tile", None),
        P(None, "lev"),
        P(None, "tile"),
        P("tile"),
        P("tile", None),
        P("tile", None),
        P("tile"),
    )
    return jax.shard_map(
        body,
        mesh=mesh,
        in_specs=placed,
        out_specs=(P(None, "tile"), P(None, "lev", "tile", None)),
        check_vma=False,
    )
```

```python
import jax
import jax.numpy as jnp
from jax import lax
from jax.experimental import pallas as pl
from jax.experimental.pallas import tpu as pltpu
from jax.sharding import PartitionSpec as P

MESH = pl.DeviceIdType.MESH
F32, BF16, I32 = jnp.float32, jnp.bfloat16, jnp.int32
NT = (((1,), (1,)), ((), ()))
TR, LV, LON, LAT, KIND = 3, 6, 32, 384, 8
EXT = LV + 4
ROWS = TR * KIND * LON
PER = KIND * LON
NTILE, NLEV, CAP, SND, FOOT = 32, 8, 64, 1024, 4
SLOTS = NTILE * CAP
CHUNK = SLOTS // NLEV
LOOK = FOOT * CHUNK


def parts_of(x, count):
    pieces = []
    for _ in range(count):
        piece = x.astype(BF16)
        pieces.append(piece)
        x = x - piece.astype(F32)
    return pieces


def onehot(rows, index, base=0):
    shape = (rows, index.shape[1])
    return (lax.broadcasted_iota(I32, shape, 0) + base == index).astype(F32)


def unrolled(low, high, body):
    for i in range(low, high):
        body(i)


def loop(low, high, body):
    def step(i, carry):
        body(i)
        return carry

    lax.fori_loop(low, high, step, 0)


def kernel(
    conc, u_in, v_in, k_in, kern_in, observed_in, weight_in, column_in, feet_in, kinds_in,
    residual, gradient,
    kern, observed, weight, column, feet, kinds, x0, x1, x2, x3, u, v, k, lon_out, lon_in, edge_u, diag_in, edge_y, kern_all, kern_wide, fields,
    ids_out, ids_in, hot, fb, kindhot, code, lathot, lonhot, cellhot, spread,
    e, picked, part_out, part_in, res, ret_in, terms, total,
    local_sem, lev_ss, lev_rs, diag_ss, diag_rs, lon_ss, lon_rs, ids_ss, ids_rs, part_ss, part_rs, ret_ss, ret_rs,
):
    tile, lev = lax.axis_index("tile"), lax.axis_index("lev")
    east, west = lax.rem(tile + 1, NTILE), lax.rem(tile + NTILE - 1, NTILE)
    above, below = lax.rem(lev + 1, NLEV), lax.rem(lev + NLEV - 1, NLEV)

    def remote(src, dst, ss, rs, target):
        return pltpu.make_async_remote_copy(
            src_ref=src, dst_ref=dst, send_sem=ss, recv_sem=rs, device_id=target, device_id_type=MESH
        )

    barrier = pltpu.get_barrier_semaphore()

    def greet(target):
        pl.semaphore_signal(barrier, inc=1, device_id=target, device_id_type=MESH)

    loop(1, NLEV, lambda d: greet({"lev": lax.rem(lev + d, NLEV)}))
    loop(1, NTILE, lambda d: greet({"tile": lax.rem(tile + d, NTILE)}))
    greet({"tile": west, "lev": below})
    greet({"tile": west, "lev": above})
    own = pl.ds(2, LV)
    loads = [
        pltpu.make_async_copy(conc, x0.at[:, own], local_sem.at[0]),
        pltpu.make_async_copy(u_in, u.at[pl.ds(1, LV)], local_sem.at[1]),
        pltpu.make_async_copy(v_in, v.at[pl.ds(1, LV)], local_sem.at[2]),
        pltpu.make_async_copy(k_in, k.at[own], local_sem.at[3]),
    ]
    small = [(kern_in, kern), (observed_in, observed), (weight_in, weight), (column_in, column), (feet_in, feet), (kinds_in, kinds)]
    smalls = [pltpu.make_async_copy(src, dst, local_sem.at[4 + n]) for n, (src, dst) in enumerate(small)]
    for copy in smalls + loads:
        copy.start()
    for copy in smalls:
        copy.wait()

    half = lax.broadcasted_iota(I32, (8, 128), 1) < CAP

    foot = feet[...]
    foot_lon = lax.shift_right_logical(lax.shift_right_logical(foot, 7) * 171, 9)
    fields[0:4, :] = (foot - foot_lon * LAT).astype(F32)
    fields[4:8, :] = foot_lon.astype(F32)
    fields[8:9, :] = kinds[...].astype(F32)
    fields[9:12, :] = observed[...]
    fields[12:13, :] = weight[...]
    fields[13:16, :] = jnp.zeros((3, SND), F32)
    target = column[...]
    match = onehot(NTILE, target)
    earlier = (
        lax.broadcasted_iota(I32, (SND, SND), 0) < lax.broadcasted_iota(I32, (SND, SND), 1)
    ).astype(F32).astype(BF16)
    before = jnp.dot(match.astype(BF16), earlier, preferred_element_type=F32)
    slot = target * CAP + jnp.sum(before * match, axis=0, keepdims=True).astype(I32)
    data = jnp.concatenate([p.astype(F32) for p in parts_of(fields[...], 3)], axis=0).astype(BF16)

    def pack(i):
        rows = pl.ds(pl.multiple_of(i * CHUNK, CHUNK), CHUNK)
        hot[rows, :] = onehot(CHUNK, slot, i * CHUNK).astype(BF16)
        got = lax.dot_general(data, hot[rows, :], NT, preferred_element_type=F32)
        got = got[0:16] + got[16:32] + got[32:48]
        for h in range(2):
            a, b = got[0:8, h * 128 : h * 128 + 128], got[8:16, h * 128 : h * 128 + 128]
            ids_out[i * 4 + h * 2] = jnp.where(half, a, pltpu.roll(b, CAP, 1))
            ids_out[i * 4 + h * 2 + 1] = jnp.where(half, pltpu.roll(a, CAP, 1), b)

    loop(0, NLEV, pack)
    ids_in[tile] = ids_out[tile]
    kern_all[0, :, 0:LV] = kern[...]

    blank = jnp.zeros((TR, LON, LAT), F32)
    x0[:, 1], x0[:, 8] = blank, blank
    x1[:, 0], x1[:, 9] = blank, blank

    def lon_copies(i):
        rows = pl.ds(0, 48 if i else 32)
        return [
            remote(
                lon_out.at[i, side, rows], lon_in.at[i, side, rows], lon_ss.at[i, side], lon_rs.at[i, side], {"tile": to}
            )
            for side, to in enumerate((east, west))
        ]

    def stage_lon(x, i, low, high):
        def one(n):
            for t in range(TR):
                lon_out[i, 0, t * 8 + n - 1] = x[t, n, LON - 1]
                lon_out[i, 1, t * 8 + n - 1] = x[t, n, 0]
                if i == 2:
                    lon_out[i, 0, 23 + t * 8 + n] = x[t, n, LON - 2]
                    lon_out[i, 1, 23 + t * 8 + n] = x[t, n, 1]
            if i == 0:
                lon_out[i, 0, 23 + n] = u[n - 1, LON - 1]

        unrolled(low, high, one)

    def stage_winds(n):
        lon_out[1, 0, 23 + n] = u[n - 1, LON - 2]
        lon_out[1, 1, 23 + n] = u[n - 1, 0]
        lon_out[1, 0, 31 + n] = v[n - 1, LON - 1]
        lon_out[1, 1, 31 + n] = v[n - 1, 0]
        lon_out[1, 0, 39 + n] = k[n, LON - 1]
        lon_out[1, 1, 39 + n] = k[n, 0]

    def finish_lon(i):
        for copy in lons[i]:
            copy.wait_recv()

        @pl.when(tile == NTILE - 1)
        def _():
            lon_in[i, 1] = jnp.zeros((48, LAT), F32)

    for copy in loads:
        copy.wait()
    stage_lon(x0, 0, 2, 8)

    lev_moves = [
        (k.at[pl.ds(LV, 2)], k.at[pl.ds(0, 2)], above),
        (kern_all.at[0], kern_all.at[1], above),
        (kern_all.at[0], kern_all.at[2], below),
        (u.at[LV], u.at[0], above),
        (u.at[1], u.at[LV + 1], below),
        (v.at[LV], v.at[0], above),
        (v.at[1], v.at[LV + 1], below),
        (k.at[2], k.at[LV + 2], below),
    ]
    lev_copies = [
        remote(src, dst, lev_ss.at[n], lev_rs.at[n], {"lev": to}) for n, (src, dst, to) in enumerate(lev_moves)
    ]
    lons = [lon_copies(0)]
    diag_copies = [
        remote(
            lon_out.at[0, 0, pl.ds(24, 8)], diag_in.at[n], diag_ss.at[n], diag_rs.at[n], {"tile": east, "lev": to}
        )
        for n, to in enumerate((above, below))
    ]

    def ids_copy(d):
        peer = lax.rem(tile + d, NTILE)
        return remote(ids_out.at[peer], ids_in.at[tile], ids_ss.at[d], ids_rs.at[d], {"tile": peer})

    def ids_wait(source):
        d = lax.rem(tile + NTILE - source, NTILE)
        remote(ids_out.at[source], ids_in.at[source], ids_ss.at[d], ids_rs.at[d], {"tile": source}).wait_recv()

    pl.semaphore_wait(barrier, NTILE - 1 + NLEV - 1 + 2)
    for copy in lons[0] + lev_copies[0:1]:
        copy.start()
    loop(1, NTILE, lambda d: ids_copy(d).start())
    for copy in diag_copies + lev_copies[1:]:
        copy.start()

    last_row = lax.broadcasted_iota(I32, (LON, LAT), 0) == LON - 1
    first_row = lax.broadcasted_iota(I32, (LON, LAT), 0) == 0
    open_face = lax.broadcasted_iota(I32, (LON, LAT), 1) < LAT - 1

    def sweep(x, i, adjoint, low, high, put):
        def one(n):
            ul, kl, kb = u[n - 1], k[n], k[n - 1]
            uw = jnp.where(first_row, edge_u[pl.ds(n - 1, 1), :], pltpu.roll(ul, 1, 0))
            vl = jnp.where(open_face, v[n - 1], 0.0)
            a, bw = jnp.maximum(ul, 0.0), jnp.minimum(uw, 0.0)
            p, q = jnp.maximum(vl, 0.0), jnp.minimum(vl, 0.0)
            if adjoint:
                qs = pltpu.roll(q, 1, 1)
            else:
                b, aw = jnp.minimum(ul, 0.0), jnp.maximum(uw, 0.0)
            for t in range(TR):
                row = pl.ds(t * 8 + n - 1, 1)
                c = x[t, n]
                ce, cw = pltpu.roll(c, LON - 1, 0), pltpu.roll(c, 1, 0)
                if i != 2:
                    edges = edge_y if i == 3 else lon_in.at[i]
                    ce = jnp.where(last_row, edges[1, row, :], ce)
                    cw = jnp.where(first_row, edges[0, row, :], cw)
                cn = pltpu.roll(c, LAT - 1, 1)
                vert = kl * (x[t, n + 1] - c) - kb * (c - x[t, n - 1])
                if adjoint:
                    cs = pltpu.roll(c, 1, 1)
                    y = c + (a * (ce - c) + bw * (c - cw)) + (p * (cn - c) + qs * (c - cs)) + vert
                else:
                    fn = p * c + q * cn
                    y = c - (a * c + b * ce) + (aw * cw + bw * c) - fn + pltpu.roll(fn, 1, 1) + vert
                put(t, n, y)

        loop(low, high, one)

    def put_in(x):
        def put(t, n, y):
            x[t, n] = y

        return put

    lev_copies[0].wait_recv()

    @pl.when(lev == 0)
    def _():
        k[0:2] = jnp.zeros((2, LON, LAT), F32)

    finish_lon(0)
    edge_u[...] = lon_in[0, 0, 24:32]

    @pl.when(tile == 0)
    def _():
        edge_u[...] = jnp.zeros((8, LAT), F32)

    sweep(x0, 0, False, 2, 8, put_in(x1))
    for t in range(TR):
        x1[t, 1] = k[1] * x0[t, 2]
        x1[t, 8] = k[7] * x0[t, 7]

    @pl.when(lev == NLEV - 1)
    def _():
        x1[:, 8] = blank

    stage_lon(x1, 1, 1, 9)
    loop(2, 8, stage_winds)
    lon_out[1, 0, 40] = k[1, LON - 1]
    lon_out[1, 1, 40] = k[1, 0]
    lons.append(lon_copies(1))
    for copy in lons[1]:
        copy.start()

    def unpack(i):
        c = lax.rem(tile // 4 + i, NLEV)
        for n in range(4):
            source = c * 4 + n

            @pl.when(source != tile)
            def _():
                ids_wait(source)

        left, right = [], []
        for h in range(2):
            a, b = ids_in[c * 4 + h * 2], ids_in[c * 4 + h * 2 + 1]
            left.append(jnp.where(half, a, pltpu.roll(b, CAP, 1)))
            right.append(jnp.where(half, pltpu.roll(a, CAP, 1), b))
        ga, gb = jnp.concatenate(left, axis=1), jnp.concatenate(right, axis=1)
        fb[c] = gb
        ga = ga.astype(I32)
        kind = gb[0:1, :].astype(I32)
        kindhot[c] = onehot(KIND, kind)
        code[c] = kind * LON + ga[4:8, :]
        for j in range(FOOT):
            cols = slice(j * CHUNK, (j + 1) * CHUNK)
            lat = onehot(LAT, ga[j : j + 1, :]).astype(BF16)
            lathot[c, 0:LAT, cols] = lat
            lathot[c, LAT : 2 * LAT, cols] = lat
            lonhot[c, :, cols] = onehot(LON, ga[4 + j : 5 + j, :])

    loop(0, NLEV, unpack)

    for copy in lev_copies[1:] + diag_copies:
        copy.wait_recv()
    edge_u[0:1] = diag_in[0, 6:7]
    edge_u[7:8] = diag_in[1, 1:2]

    @pl.when(tile == 0)
    def _():
        edge_u[...] = jnp.zeros((8, LAT), F32)

    @pl.when(lev == 0)
    def _():
        kern_all[1] = jnp.zeros((KIND, 128), F32)

    @pl.when(lev == NLEV - 1)
    def _():
        kern_all[2] = jnp.zeros((KIND, 128), F32)

    for n in range(EXT):
        which, col = (1, 4 + n) if n < 2 else (0, n - 2) if n < 8 else (2, n - 8)
        kern_wide[n] = jnp.broadcast_to(kern_all[which, :, col : col + 1], (KIND, 128))

    finish_lon(1)
    sweep(x1, 1, False, 1, 9, put_in(x2))
    for t in range(TR):
        x2[t, 0] = k[0] * x1[t, 1]
        x2[t, 9] = k[8] * x1[t, 8]

    def profile(i):
        t, h = i // 2, lax.rem(i, 2)
        rows = pl.ds(pl.multiple_of(h * 16, 16), 16)
        for w in range(LAT // 128):
            cols = slice(w * 128, (w + 1) * 128)
            planes = [x2[t, n, rows, cols] for n in range(EXT)]
            for j in range(KIND):
                acc = planes[0] * kern_wide[0, j : j + 1, :]
                for n in range(1, EXT):
                    acc = acc + planes[n] * kern_wide[n, j : j + 1, :]
                high, low = parts_of(acc, 2)
                to = pl.ds(pl.multiple_of(t * PER + j * LON + h * 16, 16), 16)
                e[to, cols] = high
                e[to, LAT + w * 128 : LAT + (w + 1) * 128] = low

    loop(0, 2 * TR, profile)

    def part_copy(c, d):
        peer = lax.rem(lev + d, NLEV)
        return remote(part_out.at[c], part_in.at[lev, c], part_ss.at[c, d], part_rs.at[c, d], {"lev": peer})

    def part_wait(c, d):
        source = lax.rem(lev + NLEV - d, NLEV)
        remote(
            part_out.at[c], part_in.at[source, c], part_ss.at[c, d], part_rs.at[c, d], {"lev": source}
        ).wait_recv()

    def gather(c):
        picked[...] = jnp.dot(e[...], lathot[c], preferred_element_type=F32)
        for j in range(FOOT):
            cellhot[c, :, j * CHUNK : (j + 1) * CHUNK] = onehot(PER, code[c, j : j + 1, :]).astype(BF16)
        mask = lonhot[c]
        for t in range(TR):
            acc = jnp.zeros((LON, CHUNK), F32)
            for j in range(KIND):
                r = t * PER + j * LON
                block = picked[r : r + LON, :] * mask
                block = (block[:, 0:CHUNK] + block[:, CHUNK : 2 * CHUNK]) + (
                    block[:, 2 * CHUNK : 3 * CHUNK] + block[:, 3 * CHUNK :]
                )
                acc = acc + block * kindhot[c, j : j + 1, :]
            row = jnp.sum(acc, axis=0, keepdims=True)
            part_out[c, t : t + 1, :] = row[:, 0:128]
            part_out[c, 3 + t : 4 + t, :] = row[:, 128:256]
        part_in[lev, c] = part_out[c]
        for d in range(1, NLEV):
            part_copy(c, d).start()

    loop(0, NLEV, gather)

    def ret_copy(peer):
        d = lax.rem(peer + NTILE - tile, NTILE)
        return remote(res.at[peer // 4], ret_in.at[tile], ret_ss.at[d], ret_rs.at[d], {"tile": peer})

    def ret_wait(d):
        source = lax.rem(tile + NTILE - d, NTILE)
        remote(res.at[source // 4], ret_in.at[source], ret_ss.at[d], ret_rs.at[d], {"tile": source}).wait_recv()

    total[...] = jnp.zeros((PER, 2 * TR * LAT), F32)

    def settle(c):
        for d in range(1, NLEV):
            part_wait(c, d)
        model = part_in[0, c]
        for z in range(1, NLEV):
            model = model + part_in[z, c]
        seen = jnp.concatenate([fb[c, 1:4, 0:128], fb[c, 1:4, 128:256]], axis=0)
        res[c, 0:6] = model[0:6] * (1.0 / FOOT) - seen
        for n in range(4):
            peer = c * 4 + n

            @pl.when(peer != tile)
            def _():
                ret_copy(peer).start()

    ahead = 3
    loop(0, ahead, settle)

    def scatter(c):
        @pl.when(c < NLEV - ahead)
        def _():
            settle(c + ahead)

        for t in range(TR):
            row = jnp.concatenate([res[c, t : t + 1, :], res[c, 3 + t : 4 + t, :]], axis=1)
            row = row * fb[c, 4:5, :] * (1.0 / FOOT)
            for h, piece in enumerate(parts_of(row, 2)):
                value = jnp.broadcast_to(piece.astype(F32), (16, CHUNK)).astype(BF16)
                value = jnp.concatenate([value] * FOOT, axis=1)
                for r in range(0, LAT, 16):
                    terms[t, h * LAT + r : h * LAT + r + 16, :] = lathot[c, r : r + 16, :] * value
            cols = slice(t * 2 * LAT, (t + 1) * 2 * LAT)
            total[:, cols] += lax.dot_general(cellhot[c], terms[t], NT, preferred_element_type=F32)

    loop(0, NLEV, scatter)
    ret_in[tile] = res[tile // 4]

    def force(h):
        rows = pl.ds(pl.multiple_of(h * 8, 8), 8)
        for t in range(TR):
            for w in range(LAT // 128):
                cols = slice(w * 128, (w + 1) * 128)
                start_high = t * 2 * LAT + w * 128
                high, low = slice(start_high, start_high + 128), slice(start_high + LAT, start_high + LAT + 128)
                sums = []
                for j in range(KIND):
                    cells = pl.ds(pl.multiple_of(j * LON + h * 8, 8), 8)
                    sums.append(total[cells, high] + total[cells, low])
                for n in range(EXT):
                    acc = sums[0] * kern_wide[n, 0:1, :]
                    for j in range(1, KIND):
                        acc = acc + sums[j] * kern_wide[n, j : j + 1, :]
                    x2[t, n, rows, cols] = acc

    loop(0, 2, lambda i: force(i * 3))
    stage_lon(x2, 2, 1, 9)
    lons.append(lon_copies(2))
    for copy in lons[2]:
        copy.start()
    loop(1, 3, force)

    sweep(x2, 2, True, 1, 9, put_in(x3))

    loop(1, NTILE, ret_wait)
    pair_odd, odd = lax.rem(tile // 2, 2) == 1, lax.rem(tile, 2) == 1
    keep = lax.broadcasted_iota(I32, (8, 128), 0) < TR

    def regroup(i):
        halves = []
        for h in range(2):
            got = ret_in[2 * i + h]
            got = jnp.where(pair_odd, pltpu.roll(got, 5, 0), got)
            moved = pltpu.roll(got, CAP, 1)
            halves.append(jnp.where(odd, got, moved) if h else jnp.where(odd, moved, got))
        both = jnp.where(half, halves[0], halves[1])
        cols = pl.ds(pl.multiple_of(i * 128, 128), 128)
        for j, piece in enumerate(parts_of(jnp.where(keep, both, 0.0), 3)):
            spread[j * 8 : j * 8 + 8, cols] = piece.astype(F32)

    loop(0, NTILE // 2, regroup)
    back = jnp.concatenate([spread[...], jnp.zeros((8, SLOTS), F32)], axis=0).astype(BF16)
    back = jnp.dot(back, hot[...], preferred_element_type=F32)
    residual[...] = (back[0:8] + back[8:16] + back[16:24])[0:TR]

    finish_lon(2)
    lane = lax.broadcasted_iota(I32, (8, LAT), 1) < LAT - 1
    here_u = edge_u[...]
    east_u = jnp.concatenate([u[n, LON - 1 : LON, :] for n in range(8)], axis=0)
    for side in range(2):
        wind = lon_in[1, side, 24:32, :]
        right, left = (here_u, wind) if side == 0 else (wind, east_u)
        north = jnp.where(lane, lon_in[1, side, 32:40, :], 0.0)
        up_k = lon_in[1, side, 40:48, :]
        low_k = pltpu.roll(up_k, 1, 0)
        a, bw = jnp.maximum(right, 0.0), jnp.minimum(left, 0.0)
        p, qs = jnp.maximum(north, 0.0), pltpu.roll(jnp.minimum(north, 0.0), 1, 1)
        for t in range(TR):
            c = lon_in[2, side, t * 8 : t * 8 + 8, :]
            far = lon_in[2, side, 24 + t * 8 : 32 + t * 8, :]
            near = jnp.concatenate([x2[t, n, side * (LON - 1) : side * (LON - 1) + 1, :] for n in range(1, 9)], axis=0)
            ce, cw = (near, far) if side == 0 else (far, near)
            cn, cs = pltpu.roll(c, LAT - 1, 1), pltpu.roll(c, 1, 1)
            vert = up_k * (pltpu.roll(c, 7, 0) - c) - low_k * (c - pltpu.roll(c, 1, 0))
            edge_y[side, t * 8 : t * 8 + 8, :] = (
                c + (a * (ce - c) + bw * (c - cw)) + (p * (cn - c) + qs * (c - cs)) + vert
            )

    top, bottom = lax.broadcasted_iota(I32, (8, LAT), 0) == 7, lax.broadcasted_iota(I32, (8, LAT), 0) == 0

    def column(ref, at, low=0):
        return jnp.concatenate([ref[n, at : at + 1, :] for n in range(low, low + 8)], axis=0)

    for side in range(2):
        at = side * (LON - 1)
        right, left = (column(u, 0), here_u) if side == 0 else (east_u, column(u, LON - 2))
        north = jnp.where(lane, column(v, at), 0.0)
        up_k, low_k = column(k, at, 1), column(k, at)
        a, bw = jnp.maximum(right, 0.0), jnp.minimum(left, 0.0)
        p, qs = jnp.maximum(north, 0.0), pltpu.roll(jnp.minimum(north, 0.0), 1, 1)
        for t in range(TR):
            c = lon_out[2, 1 - side, t * 8 : t * 8 + 8, :]
            near = lon_out[2, 1 - side, 24 + t * 8 : 32 + t * 8, :]
            far = lon_in[2, side, t * 8 : t * 8 + 8, :]
            ce, cw = (near, far) if side == 0 else (far, near)
            cn, cs = pltpu.roll(c, LAT - 1, 1), pltpu.roll(c, 1, 1)
            up = jnp.where(top, x2[t, 9, at : at + 1, :], pltpu.roll(c, 7, 0))
            low = jnp.where(bottom, x2[t, 0, at : at + 1, :], pltpu.roll(c, 1, 0))
            vert = up_k * (up - c) - low_k * (c - low)
            y = c + (a * (ce - c) + bw * (c - cw)) + (p * (cn - c) + qs * (c - cs)) + vert
            for n in range(8):
                x3[t, n + 1, at : at + 1, :] = y[n : n + 1, :]

    @pl.when(lev == NLEV - 1)
    def _():
        x3[:, 8] = blank

    @pl.when(tile == NTILE - 1)
    def _():
        edge_y[1] = jnp.zeros((24, LAT), F32)

    def put_gradient(t, n, y):
        gradient[t, n - 2] = y

    sweep(x3, 3, True, 2, 8, put_gradient)

    for copies in lons + [lev_copies, diag_copies]:
        for copy in copies:
            copy.wait_send()
    unrolled(1, NTILE, lambda d: ids_copy(d).wait_send())
    unrolled(1, NTILE, lambda d: ret_copy(lax.rem(tile + d, NTILE)).wait_send())

    def parts_sent(c):
        for d in range(1, NLEV):
            part_copy(c, d).wait_send()

    loop(0, NLEV, parts_sent)


def store(a, b, a_out, b_out, a_held, b_held, in_sem, out_sem):
    into = [pltpu.make_async_copy(b.at[t], b_held.at[t], in_sem.at[t]) for t in range(TR)]
    out = [pltpu.make_async_copy(b_held.at[t], b_out.at[t], out_sem.at[t]) for t in range(TR)]
    into.append(pltpu.make_async_copy(a, a_held, in_sem.at[TR]))
    out.append(pltpu.make_async_copy(a_held, a_out, out_sem.at[TR]))
    for copy in into:
        copy.start()
    for got, put in zip(into, out):
        got.wait()
        put.start()
    for copy in out:
        copy.wait()


def body(conc, u_wind, v_wind, mixing, kernels, observed, obs_weight, column_tile, footprint, kernel_index):
    dma = pltpu.SemaphoreType.DMA
    hbm, vmem = pl.BlockSpec(memory_space=pl.ANY), pl.BlockSpec(memory_space=pltpu.VMEM)
    ext = pltpu.VMEM((TR, EXT, LON, LAT), F32)
    shapes = (
        jax.ShapeDtypeStruct((TR, SND), F32),
        jax.ShapeDtypeStruct((TR, LV, LON, LAT), F32),
    )
    found = pl.pallas_call(
        kernel,
        out_shape=shapes,
        in_specs=[hbm] * 10,
        out_specs=(vmem, vmem),
        scratch_shapes=[
            pltpu.VMEM((KIND, LV), F32),
            pltpu.VMEM((TR, SND), F32),
            pltpu.VMEM((1, SND), F32),
            pltpu.VMEM((1, SND), I32),
            pltpu.VMEM((FOOT, SND), I32),
            pltpu.VMEM((1, SND), I32),
            ext, ext, ext, ext,
            pltpu.VMEM((LV + 2, LON, LAT), F32),
            pltpu.VMEM((LV + 2, LON, LAT), F32),
            pltpu.VMEM((LV + 3, LON, LAT), F32),
            pltpu.VMEM((3, 2, 48, LAT), F32),
            pltpu.VMEM((3, 2, 48, LAT), F32),
            pltpu.VMEM((8, LAT), F32),
            pltpu.VMEM((2, 8, LAT), F32),
            pltpu.VMEM((2, 24, LAT), F32),
            pltpu.VMEM((3, KIND, 128), F32),
            pltpu.VMEM((EXT, KIND, 128), F32),
            pltpu.VMEM((16, SND), F32),
            pltpu.VMEM((NTILE, 8, 128), F32),
            pltpu.VMEM((NTILE, 8, 128), F32),
            pltpu.VMEM((SLOTS, SND), BF16),
            pltpu.VMEM((NLEV, 8, CHUNK), F32),
            pltpu.VMEM((NLEV, KIND, CHUNK), F32),
            pltpu.VMEM((NLEV, FOOT, CHUNK), I32),
            pltpu.VMEM((NLEV, 2 * LAT, LOOK), BF16),
            pltpu.VMEM((NLEV, LON, LOOK), F32),
            pltpu.VMEM((NLEV, PER, LOOK), BF16),
            pltpu.VMEM((24, SLOTS), F32),
            pltpu.VMEM((ROWS, 2 * LAT), BF16),
            pltpu.VMEM((ROWS, LOOK), F32),
            pltpu.VMEM((NLEV, 8, 128), F32),
            pltpu.VMEM((NLEV, NLEV, 8, 128), F32),
            pltpu.VMEM((NLEV, 8, 128), F32),
            pltpu.VMEM((NTILE, 8, 128), F32),
            pltpu.VMEM((TR, 2 * LAT, LOOK), BF16),
            pltpu.VMEM((PER, 2 * TR * LAT), F32),
            dma((10,)),
            dma((8,)), dma((8,)),
            dma((2,)), dma((2,)),
            dma((3, 2)), dma((3, 2)),
            dma((NTILE,)), dma((NTILE,)),
            dma((NLEV, NLEV)), dma((NLEV, NLEV)),
            dma((NTILE,)), dma((NTILE,)),
        ],
        compiler_params=pltpu.CompilerParams(
            collective_id=0, has_side_effects=True, vmem_limit_bytes=60 * 1024 * 1024
        ),
    )(
        conc, u_wind, v_wind, mixing, kernels, observed, obs_weight[None], column_tile.T, footprint.T, kernel_index[None]
    )
    return pl.pallas_call(
        store,
        out_shape=shapes,
        in_specs=[hbm] * 2,
        out_specs=(hbm, hbm),
        scratch_shapes=[
            pltpu.VMEM((TR, SND), F32),
            pltpu.VMEM((TR, LV, LON, LAT), F32),
            dma((TR + 1,)),
            dma((TR + 1,)),
        ],
        compiler_params=pltpu.CompilerParams(vmem_limit_bytes=60 * 1024 * 1024),
    )(*found)


def solution(mesh):
    placed = (
        P(None, "lev", "tile", None),
        P("lev", "tile", None),
        P("lev", "tile", None),
        P("lev", "tile", None),
        P(None, "lev"),
        P(None, "tile"),
        P("tile"),
        P("tile", None),
        P("tile", None),
        P("tile"),
    )
    return jax.shard_map(
        body,
        mesh=mesh,
        in_specs=placed,
        out_specs=(P(None, "tile"), P(None, "lev", "tile", None)),
        check_vma=False,
    )
```

```python
import jax
import jax.numpy as jnp
from jax import lax
from jax.experimental import pallas as pl
from jax.experimental.pallas import tpu as pltpu
from jax.sharding import PartitionSpec as P

MESH = pl.DeviceIdType.MESH
F32, BF16, I32 = jnp.float32, jnp.bfloat16, jnp.int32
NT = (((1,), (1,)), ((), ()))
TR, LV, LON, LAT, KIND = 3, 6, 32, 384, 8
EXT = LV + 4
ROWS = TR * KIND * LON
PER = KIND * LON
NTILE, NLEV, CAP, SND, FOOT = 32, 8, 64, 1024, 4
SLOTS = NTILE * CAP
CHUNK = SLOTS // NLEV
LOOK = FOOT * CHUNK


def parts_of(x, count):
    pieces = []
    for _ in range(count):
        piece = x.astype(BF16)
        pieces.append(piece)
        x = x - piece.astype(F32)
    return pieces


def onehot(rows, index, base=0):
    shape = (rows, index.shape[1])
    return (lax.broadcasted_iota(I32, shape, 0) + base == index).astype(F32)


def unrolled(low, high, body):
    for i in range(low, high):
        body(i)


def loop(low, high, body):
    def step(i, carry):
        body(i)
        return carry

    lax.fori_loop(low, high, step, 0)


def kernel(
    conc, u_in, v_in, k_in, kern_in, observed_in, weight_in, column_in, feet_in, kinds_in,
    residual, gradient,
    kern, observed, weight, column, feet, kinds, x0, x1, x2, x3, u, v, k, lon_out, lon_in, edge_u, diag_in, edge_y, kern_all, kern_wide, fields,
    ids_out, ids_in, hot, fb, kindhot, code, lathot, lonhot, cellhot, spread,
    e, picked, part_out, part_in, res, ret_in, terms, total,
    local_sem, lev_ss, lev_rs, diag_ss, diag_rs, lon_ss, lon_rs, ids_ss, ids_rs, part_ss, part_rs, ret_ss, ret_rs,
):
    tile, lev = lax.axis_index("tile"), lax.axis_index("lev")
    east, west = lax.rem(tile + 1, NTILE), lax.rem(tile + NTILE - 1, NTILE)
    above, below = lax.rem(lev + 1, NLEV), lax.rem(lev + NLEV - 1, NLEV)

    def remote(src, dst, ss, rs, target):
        return pltpu.make_async_remote_copy(
            src_ref=src, dst_ref=dst, send_sem=ss, recv_sem=rs, device_id=target, device_id_type=MESH
        )

    barrier = pltpu.get_barrier_semaphore()

    def greet(target):
        pl.semaphore_signal(barrier, inc=1, device_id=target, device_id_type=MESH)

    loop(1, NLEV, lambda d: greet({"lev": lax.rem(lev + d, NLEV)}))
    loop(1, NTILE, lambda d: greet({"tile": lax.rem(tile + d, NTILE)}))
    greet({"tile": west, "lev": below})
    greet({"tile": west, "lev": above})
    own = pl.ds(2, LV)
    loads = [
        pltpu.make_async_copy(conc, x0.at[:, own], local_sem.at[0]),
        pltpu.make_async_copy(u_in, u.at[pl.ds(1, LV)], local_sem.at[1]),
        pltpu.make_async_copy(v_in, v.at[pl.ds(1, LV)], local_sem.at[2]),
        pltpu.make_async_copy(k_in, k.at[own], local_sem.at[3]),
    ]
    small = [(kern_in, kern), (observed_in, observed), (weight_in, weight), (column_in, column), (feet_in, feet), (kinds_in, kinds)]
    smalls = [pltpu.make_async_copy(src, dst, local_sem.at[4 + n]) for n, (src, dst) in enumerate(small)]
    for copy in smalls + loads:
        copy.start()
    for copy in smalls:
        copy.wait()

    half = lax.broadcasted_iota(I32, (8, 128), 1) < CAP

    foot = feet[...]
    foot_lon = lax.shift_right_logical(lax.shift_right_logical(foot, 7) * 171, 9)
    fields[0:4, :] = (foot - foot_lon * LAT).astype(F32)
    fields[4:8, :] = foot_lon.astype(F32)
    fields[8:9, :] = kinds[...].astype(F32)
    fields[9:12, :] = observed[...]
    fields[12:13, :] = weight[...]
    fields[13:16, :] = jnp.zeros((3, SND), F32)
    target = column[...]
    match = onehot(NTILE, target)
    earlier = (
        lax.broadcasted_iota(I32, (SND, SND), 0) < lax.broadcasted_iota(I32, (SND, SND), 1)
    ).astype(F32).astype(BF16)
    before = jnp.dot(match.astype(BF16), earlier, preferred_element_type=F32)
    slot = target * CAP + jnp.sum(before * match, axis=0, keepdims=True).astype(I32)
    data = jnp.concatenate([p.astype(F32) for p in parts_of(fields[...], 3)], axis=0).astype(BF16)

    def pack(i):
        rows = pl.ds(pl.multiple_of(i * CHUNK, CHUNK), CHUNK)
        hot[rows, :] = onehot(CHUNK, slot, i * CHUNK).astype(BF16)
        got = lax.dot_general(data, hot[rows, :], NT, preferred_element_type=F32)
        got = got[0:16] + got[16:32] + got[32:48]
        for h in range(2):
            a, b = got[0:8, h * 128 : h * 128 + 128], got[8:16, h * 128 : h * 128 + 128]
            ids_out[i * 4 + h * 2] = jnp.where(half, a, pltpu.roll(b, CAP, 1))
            ids_out[i * 4 + h * 2 + 1] = jnp.where(half, pltpu.roll(a, CAP, 1), b)

    loop(0, NLEV, pack)
    ids_in[tile] = ids_out[tile]
    kern_all[0, :, 0:LV] = kern[...]

    blank = jnp.zeros((TR, LON, LAT), F32)
    x0[:, 1], x0[:, 8] = blank, blank
    x1[:, 0], x1[:, 9] = blank, blank

    def lon_copies(i):
        rows = pl.ds(0, 48 if i else 32)
        return [
            remote(
                lon_out.at[i, side, rows], lon_in.at[i, side, rows], lon_ss.at[i, side], lon_rs.at[i, side], {"tile": to}
            )
            for side, to in enumerate((east, west))
        ]

    def stage_lon(x, i, low, high):
        def one(n):
            for t in range(TR):
                lon_out[i, 0, t * 8 + n - 1] = x[t, n, LON - 1]
                lon_out[i, 1, t * 8 + n - 1] = x[t, n, 0]
                if i == 2:
                    lon_out[i, 0, 23 + t * 8 + n] = x[t, n, LON - 2]
                    lon_out[i, 1, 23 + t * 8 + n] = x[t, n, 1]
            if i == 0:
                lon_out[i, 0, 23 + n] = u[n - 1, LON - 1]

        unrolled(low, high, one)

    def stage_winds(n):
        lon_out[1, 0, 23 + n] = u[n - 1, LON - 2]
        lon_out[1, 1, 23 + n] = u[n - 1, 0]
        lon_out[1, 0, 31 + n] = v[n - 1, LON - 1]
        lon_out[1, 1, 31 + n] = v[n - 1, 0]
        lon_out[1, 0, 39 + n] = k[n, LON - 1]
        lon_out[1, 1, 39 + n] = k[n, 0]

    def finish_lon(i):
        for copy in lons[i]:
            copy.wait_recv()

        @pl.when(tile == NTILE - 1)
        def _():
            lon_in[i, 1] = jnp.zeros((48, LAT), F32)

    for copy in loads:
        copy.wait()
    stage_lon(x0, 0, 2, 8)

    lev_moves = [
        (k.at[pl.ds(LV, 2)], k.at[pl.ds(0, 2)], above),
        (kern_all.at[0], kern_all.at[1], above),
        (kern_all.at[0], kern_all.at[2], below),
        (u.at[LV], u.at[0], above),
        (u.at[1], u.at[LV + 1], below),
        (v.at[LV], v.at[0], above),
        (v.at[1], v.at[LV + 1], below),
        (k.at[2], k.at[LV + 2], below),
    ]
    lev_copies = [
        remote(src, dst, lev_ss.at[n], lev_rs.at[n], {"lev": to}) for n, (src, dst, to) in enumerate(lev_moves)
    ]
    lons = [lon_copies(0)]
    diag_copies = [
        remote(
            lon_out.at[0, 0, pl.ds(24, 8)], diag_in.at[n], diag_ss.at[n], diag_rs.at[n], {"tile": east, "lev": to}
        )
        for n, to in enumerate((above, below))
    ]

    def ids_copy(d):
        peer = lax.rem(tile + d, NTILE)
        return remote(ids_out.at[peer], ids_in.at[tile], ids_ss.at[d], ids_rs.at[d], {"tile": peer})

    def ids_wait(source):
        d = lax.rem(tile + NTILE - source, NTILE)
        remote(ids_out.at[source], ids_in.at[source], ids_ss.at[d], ids_rs.at[d], {"tile": source}).wait_recv()

    pl.semaphore_wait(barrier, NTILE - 1 + NLEV - 1 + 2)
    for copy in lons[0] + lev_copies[0:1]:
        copy.start()
    loop(1, NTILE, lambda d: ids_copy(d).start())
    for copy in diag_copies + lev_copies[1:]:
        copy.start()

    last_row = lax.broadcasted_iota(I32, (LON, LAT), 0) == LON - 1
    first_row = lax.broadcasted_iota(I32, (LON, LAT), 0) == 0
    open_face = lax.broadcasted_iota(I32, (LON, LAT), 1) < LAT - 1

    def sweep(x, i, adjoint, low, high, put):
        def one(n):
            ul, kl, kb = u[n - 1], k[n], k[n - 1]
            uw = jnp.where(first_row, edge_u[pl.ds(n - 1, 1), :], pltpu.roll(ul, 1, 0))
            vl = jnp.where(open_face, v[n - 1], 0.0)
            a, bw = jnp.maximum(ul, 0.0), jnp.minimum(uw, 0.0)
            p, q = jnp.maximum(vl, 0.0), jnp.minimum(vl, 0.0)
            if adjoint:
                qs = pltpu.roll(q, 1, 1)
            else:
                b, aw = jnp.minimum(ul, 0.0), jnp.maximum(uw, 0.0)
            for t in range(TR):
                row = pl.ds(t * 8 + n - 1, 1)
                c = x[t, n]
                ce, cw = pltpu.roll(c, LON - 1, 0), pltpu.roll(c, 1, 0)
                if i != 2:
                    edges = edge_y if i == 3 else lon_in.at[i]
                    ce = jnp.where(last_row, edges[1, row, :], ce)
                    cw = jnp.where(first_row, edges[0, row, :], cw)
                cn = pltpu.roll(c, LAT - 1, 1)
                vert = kl * (x[t, n + 1] - c) - kb * (c - x[t, n - 1])
                if adjoint:
                    cs = pltpu.roll(c, 1, 1)
                    y = c + (a * (ce - c) + bw * (c - cw)) + (p * (cn - c) + qs * (c - cs)) + vert
                else:
                    fn = p * c + q * cn
                    y = c - (a * c + b * ce) + (aw * cw + bw * c) - fn + pltpu.roll(fn, 1, 1) + vert
                put(t, n, y)

        loop(low, high, one)

    def put_in(x):
        def put(t, n, y):
            x[t, n] = y

        return put

    lev_copies[0].wait_recv()

    @pl.when(lev == 0)
    def _():
        k[0:2] = jnp.zeros((2, LON, LAT), F32)

    finish_lon(0)
    edge_u[...] = lon_in[0, 0, 24:32]

    @pl.when(tile == 0)
    def _():
        edge_u[...] = jnp.zeros((8, LAT), F32)

    sweep(x0, 0, False, 2, 8, put_in(x1))
    for t in range(TR):
        x1[t, 1] = k[1] * x0[t, 2]
        x1[t, 8] = k[7] * x0[t, 7]

    @pl.when(lev == NLEV - 1)
    def _():
        x1[:, 8] = blank

    stage_lon(x1, 1, 1, 9)
    loop(2, 8, stage_winds)
    lon_out[1, 0, 40] = k[1, LON - 1]
    lon_out[1, 1, 40] = k[1, 0]
    lons.append(lon_copies(1))
    for copy in lons[1]:
        copy.start()

    def unpack(i):
        c = lax.rem(tile // 4 + i, NLEV)
        for n in range(4):
            source = c * 4 + n

            @pl.when(source != tile)
            def _():
                ids_wait(source)

        left, right = [], []
        for h in range(2):
            a, b = ids_in[c * 4 + h * 2], ids_in[c * 4 + h * 2 + 1]
            left.append(jnp.where(half, a, pltpu.roll(b, CAP, 1)))
            right.append(jnp.where(half, pltpu.roll(a, CAP, 1), b))
        ga, gb = jnp.concatenate(left, axis=1), jnp.concatenate(right, axis=1)
        fb[c] = gb
        ga = ga.astype(I32)
        kind = gb[0:1, :].astype(I32)
        kindhot[c] = onehot(KIND, kind)
        code[c] = kind * LON + ga[4:8, :]
        for j in range(FOOT):
            cols = slice(j * CHUNK, (j + 1) * CHUNK)
            lat = onehot(LAT, ga[j : j + 1, :]).astype(BF16)
            lathot[c, 0:LAT, cols] = lat
            lathot[c, LAT : 2 * LAT, cols] = lat
            lonhot[c, :, cols] = onehot(LON, ga[4 + j : 5 + j, :])

    loop(0, NLEV, unpack)

    for copy in lev_copies[1:] + diag_copies:
        copy.wait_recv()
    edge_u[0:1] = diag_in[0, 6:7]
    edge_u[7:8] = diag_in[1, 1:2]

    @pl.when(tile == 0)
    def _():
        edge_u[...] = jnp.zeros((8, LAT), F32)

    @pl.when(lev == 0)
    def _():
        kern_all[1] = jnp.zeros((KIND, 128), F32)

    @pl.when(lev == NLEV - 1)
    def _():
        kern_all[2] = jnp.zeros((KIND, 128), F32)

    for n in range(EXT):
        which, col = (1, 4 + n) if n < 2 else (0, n - 2) if n < 8 else (2, n - 8)
        kern_wide[n] = jnp.broadcast_to(kern_all[which, :, col : col + 1], (KIND, 128))

    finish_lon(1)
    sweep(x1, 1, False, 1, 9, put_in(x2))
    for t in range(TR):
        x2[t, 0] = k[0] * x1[t, 1]
        x2[t, 9] = k[8] * x1[t, 8]

    def profile(i):
        t, h = i // 2, lax.rem(i, 2)
        rows = pl.ds(pl.multiple_of(h * 16, 16), 16)
        for w in range(LAT // 128):
            cols = slice(w * 128, (w + 1) * 128)
            planes = [x2[t, n, rows, cols] for n in range(EXT)]
            for j in range(KIND):
                acc = planes[0] * kern_wide[0, j : j + 1, :]
                for n in range(1, EXT):
                    acc = acc + planes[n] * kern_wide[n, j : j + 1, :]
                high, low = parts_of(acc, 2)
                to = pl.ds(pl.multiple_of(t * PER + j * LON + h * 16, 16), 16)
                e[to, cols] = high
                e[to, LAT + w * 128 : LAT + (w + 1) * 128] = low

    loop(0, 2 * TR, profile)

    def part_copy(c, d):
        peer = lax.rem(lev + d, NLEV)
        return remote(part_out.at[c], part_in.at[lev, c], part_ss.at[c, d], part_rs.at[c, d], {"lev": peer})

    def part_wait(c, d):
        source = lax.rem(lev + NLEV - d, NLEV)
        remote(
            part_out.at[c], part_in.at[source, c], part_ss.at[c, d], part_rs.at[c, d], {"lev": source}
        ).wait_recv()

    def gather(c):
        picked[...] = jnp.dot(e[...], lathot[c], preferred_element_type=F32)
        for j in range(FOOT):
            cellhot[c, :, j * CHUNK : (j + 1) * CHUNK] = onehot(PER, code[c, j : j + 1, :]).astype(BF16)
        mask = lonhot[c]
        for t in range(TR):
            acc = jnp.zeros((LON, CHUNK), F32)
            for j in range(KIND):
                r = t * PER + j * LON
                block = picked[r : r + LON, :] * mask
                block = (block[:, 0:CHUNK] + block[:, CHUNK : 2 * CHUNK]) + (
                    block[:, 2 * CHUNK : 3 * CHUNK] + block[:, 3 * CHUNK :]
                )
                acc = acc + block * kindhot[c, j : j + 1, :]
            row = jnp.sum(acc, axis=0, keepdims=True)
            part_out[c, t : t + 1, :] = row[:, 0:128]
            part_out[c, 3 + t : 4 + t, :] = row[:, 128:256]
        part_in[lev, c] = part_out[c]
        for d in range(1, NLEV):
            part_copy(c, d).start()

    loop(0, NLEV, gather)

    def ret_copy(peer):
        d = lax.rem(peer + NTILE - tile, NTILE)
        return remote(res.at[peer // 4], ret_in.at[tile], ret_ss.at[d], ret_rs.at[d], {"tile": peer})

    def ret_wait(d):
        source = lax.rem(tile + NTILE - d, NTILE)
        remote(res.at[source // 4], ret_in.at[source], ret_ss.at[d], ret_rs.at[d], {"tile": source}).wait_recv()

    total[...] = jnp.zeros((PER, 2 * TR * LAT), F32)

    def settle(c):
        for d in range(1, NLEV):
            part_wait(c, d)
        model = part_in[0, c]
        for z in range(1, NLEV):
            model = model + part_in[z, c]
        seen = jnp.concatenate([fb[c, 1:4, 0:128], fb[c, 1:4, 128:256]], axis=0)
        res[c, 0:6] = model[0:6] * (1.0 / FOOT) - seen
        for n in range(4):
            peer = c * 4 + n

            @pl.when(peer != tile)
            def _():
                ret_copy(peer).start()

    ahead = 3
    loop(0, ahead, settle)

    def scatter(c):
        @pl.when(c < NLEV - ahead)
        def _():
            settle(c + ahead)

        for t in range(TR):
            row = jnp.concatenate([res[c, t : t + 1, :], res[c, 3 + t : 4 + t, :]], axis=1)
            row = row * fb[c, 4:5, :] * (1.0 / FOOT)
            for h, piece in enumerate(parts_of(row, 2)):
                value = jnp.broadcast_to(piece.astype(F32), (16, CHUNK)).astype(BF16)
                value = jnp.concatenate([value] * FOOT, axis=1)
                for r in range(0, LAT, 16):
                    terms[t, h * LAT + r : h * LAT + r + 16, :] = lathot[c, r : r + 16, :] * value
            cols = slice(t * 2 * LAT, (t + 1) * 2 * LAT)
            total[:, cols] += lax.dot_general(cellhot[c], terms[t], NT, preferred_element_type=F32)

    loop(0, NLEV, scatter)
    ret_in[tile] = res[tile // 4]

    def force(h):
        rows = pl.ds(pl.multiple_of(h * 8, 8), 8)
        for t in range(TR):
            for w in range(LAT // 128):
                cols = slice(w * 128, (w + 1) * 128)
                start_high = t * 2 * LAT + w * 128
                high, low = slice(start_high, start_high + 128), slice(start_high + LAT, start_high + LAT + 128)
                sums = []
                for j in range(KIND):
                    cells = pl.ds(pl.multiple_of(j * LON + h * 8, 8), 8)
                    sums.append(total[cells, high] + total[cells, low])
                for n in range(EXT):
                    acc = sums[0] * kern_wide[n, 0:1, :]
                    for j in range(1, KIND):
                        acc = acc + sums[j] * kern_wide[n, j : j + 1, :]
                    x2[t, n, rows, cols] = acc

    loop(0, 2, lambda i: force(i * 3))
    stage_lon(x2, 2, 1, 9)
    lons.append(lon_copies(2))
    for copy in lons[2]:
        copy.start()
    loop(1, 3, force)

    sweep(x2, 2, True, 1, 9, put_in(x3))

    loop(1, NTILE, ret_wait)
    pair_odd, odd = lax.rem(tile // 2, 2) == 1, lax.rem(tile, 2) == 1
    keep = lax.broadcasted_iota(I32, (8, 128), 0) < TR

    def regroup(i):
        halves = []
        for h in range(2):
            got = ret_in[2 * i + h]
            got = jnp.where(pair_odd, pltpu.roll(got, 5, 0), got)
            moved = pltpu.roll(got, CAP, 1)
            halves.append(jnp.where(odd, got, moved) if h else jnp.where(odd, moved, got))
        both = jnp.where(half, halves[0], halves[1])
        cols = pl.ds(pl.multiple_of(i * 128, 128), 128)
        for j, piece in enumerate(parts_of(jnp.where(keep, both, 0.0), 3)):
            spread[j * 8 : j * 8 + 8, cols] = piece.astype(F32)

    loop(0, NTILE // 2, regroup)
    back = jnp.concatenate([spread[...], jnp.zeros((8, SLOTS), F32)], axis=0).astype(BF16)
    back = jnp.dot(back, hot[...], preferred_element_type=F32)
    residual[...] = (back[0:8] + back[8:16] + back[16:24])[0:TR]

    for copies in lons[0:2] + [lev_copies, diag_copies]:
        for copy in copies:
            copy.wait_send()
    unrolled(1, NTILE, lambda d: ids_copy(d).wait_send())

    def parts_sent(c):
        for d in range(1, NLEV):
            part_copy(c, d).wait_send()

    loop(0, NLEV, parts_sent)
    finish_lon(2)
    lane = lax.broadcasted_iota(I32, (8, LAT), 1) < LAT - 1
    here_u = edge_u[...]
    east_u = jnp.concatenate([u[n, LON - 1 : LON, :] for n in range(8)], axis=0)
    for side in range(2):
        wind = lon_in[1, side, 24:32, :]
        right, left = (here_u, wind) if side == 0 else (wind, east_u)
        north = jnp.where(lane, lon_in[1, side, 32:40, :], 0.0)
        up_k = lon_in[1, side, 40:48, :]
        low_k = pltpu.roll(up_k, 1, 0)
        a, bw = jnp.maximum(right, 0.0), jnp.minimum(left, 0.0)
        p, qs = jnp.maximum(north, 0.0), pltpu.roll(jnp.minimum(north, 0.0), 1, 1)
        for t in range(TR):
            c = lon_in[2, side, t * 8 : t * 8 + 8, :]
            far = lon_in[2, side, 24 + t * 8 : 32 + t * 8, :]
            near = jnp.concatenate([x2[t, n, side * (LON - 1) : side * (LON - 1) + 1, :] for n in range(1, 9)], axis=0)
            ce, cw = (near, far) if side == 0 else (far, near)
            cn, cs = pltpu.roll(c, LAT - 1, 1), pltpu.roll(c, 1, 1)
            vert = up_k * (pltpu.roll(c, 7, 0) - c) - low_k * (c - pltpu.roll(c, 1, 0))
            edge_y[side, t * 8 : t * 8 + 8, :] = (
                c + (a * (ce - c) + bw * (c - cw)) + (p * (cn - c) + qs * (c - cs)) + vert
            )

    top, bottom = lax.broadcasted_iota(I32, (8, LAT), 0) == 7, lax.broadcasted_iota(I32, (8, LAT), 0) == 0

    def column(ref, at, low=0):
        return jnp.concatenate([ref[n, at : at + 1, :] for n in range(low, low + 8)], axis=0)

    for side in range(2):
        at = side * (LON - 1)
        right, left = (column(u, 0), here_u) if side == 0 else (east_u, column(u, LON - 2))
        north = jnp.where(lane, column(v, at), 0.0)
        up_k, low_k = column(k, at, 1), column(k, at)
        a, bw = jnp.maximum(right, 0.0), jnp.minimum(left, 0.0)
        p, qs = jnp.maximum(north, 0.0), pltpu.roll(jnp.minimum(north, 0.0), 1, 1)
        for t in range(TR):
            c = lon_out[2, 1 - side, t * 8 : t * 8 + 8, :]
            near = lon_out[2, 1 - side, 24 + t * 8 : 32 + t * 8, :]
            far = lon_in[2, side, t * 8 : t * 8 + 8, :]
            ce, cw = (near, far) if side == 0 else (far, near)
            cn, cs = pltpu.roll(c, LAT - 1, 1), pltpu.roll(c, 1, 1)
            up = jnp.where(top, x2[t, 9, at : at + 1, :], pltpu.roll(c, 7, 0))
            low = jnp.where(bottom, x2[t, 0, at : at + 1, :], pltpu.roll(c, 1, 0))
            vert = up_k * (up - c) - low_k * (c - low)
            y = c + (a * (ce - c) + bw * (c - cw)) + (p * (cn - c) + qs * (c - cs)) + vert
            for n in range(8):
                x3[t, n + 1, at : at + 1, :] = y[n : n + 1, :]

    @pl.when(lev == NLEV - 1)
    def _():
        x3[:, 8] = blank

    @pl.when(tile == NTILE - 1)
    def _():
        edge_y[1] = jnp.zeros((24, LAT), F32)

    def put_gradient(t, n, y):
        gradient[t, n - 2] = y

    sweep(x3, 3, True, 2, 8, put_gradient)

    for copy in lons[2]:
        copy.wait_send()
    unrolled(1, NTILE, lambda d: ret_copy(lax.rem(tile + d, NTILE)).wait_send())


def store(a, b, a_out, b_out, a_held, b_held, in_sem, out_sem):
    into = [pltpu.make_async_copy(b.at[t], b_held.at[t], in_sem.at[t]) for t in range(TR)]
    out = [pltpu.make_async_copy(b_held.at[t], b_out.at[t], out_sem.at[t]) for t in range(TR)]
    into.append(pltpu.make_async_copy(a, a_held, in_sem.at[TR]))
    out.append(pltpu.make_async_copy(a_held, a_out, out_sem.at[TR]))
    for copy in into:
        copy.start()
    for got, put in zip(into, out):
        got.wait()
        put.start()
    for copy in out:
        copy.wait()


def body(conc, u_wind, v_wind, mixing, kernels, observed, obs_weight, column_tile, footprint, kernel_index):
    dma = pltpu.SemaphoreType.DMA
    hbm, vmem = pl.BlockSpec(memory_space=pl.ANY), pl.BlockSpec(memory_space=pltpu.VMEM)
    ext = pltpu.VMEM((TR, EXT, LON, LAT), F32)
    shapes = (
        jax.ShapeDtypeStruct((TR, SND), F32),
        jax.ShapeDtypeStruct((TR, LV, LON, LAT), F32),
    )
    found = pl.pallas_call(
        kernel,
        out_shape=shapes,
        in_specs=[hbm] * 10,
        out_specs=(vmem, vmem),
        scratch_shapes=[
            pltpu.VMEM((KIND, LV), F32),
            pltpu.VMEM((TR, SND), F32),
            pltpu.VMEM((1, SND), F32),
            pltpu.VMEM((1, SND), I32),
            pltpu.VMEM((FOOT, SND), I32),
            pltpu.VMEM((1, SND), I32),
            ext, ext, ext, ext,
            pltpu.VMEM((LV + 2, LON, LAT), F32),
            pltpu.VMEM((LV + 2, LON, LAT), F32),
            pltpu.VMEM((LV + 3, LON, LAT), F32),
            pltpu.VMEM((3, 2, 48, LAT), F32),
            pltpu.VMEM((3, 2, 48, LAT), F32),
            pltpu.VMEM((8, LAT), F32),
            pltpu.VMEM((2, 8, LAT), F32),
            pltpu.VMEM((2, 24, LAT), F32),
            pltpu.VMEM((3, KIND, 128), F32),
            pltpu.VMEM((EXT, KIND, 128), F32),
            pltpu.VMEM((16, SND), F32),
            pltpu.VMEM((NTILE, 8, 128), F32),
            pltpu.VMEM((NTILE, 8, 128), F32),
            pltpu.VMEM((SLOTS, SND), BF16),
            pltpu.VMEM((NLEV, 8, CHUNK), F32),
            pltpu.VMEM((NLEV, KIND, CHUNK), F32),
            pltpu.VMEM((NLEV, FOOT, CHUNK), I32),
            pltpu.VMEM((NLEV, 2 * LAT, LOOK), BF16),
            pltpu.VMEM((NLEV, LON, LOOK), F32),
            pltpu.VMEM((NLEV, PER, LOOK), BF16),
            pltpu.VMEM((24, SLOTS), F32),
            pltpu.VMEM((ROWS, 2 * LAT), BF16),
            pltpu.VMEM((ROWS, LOOK), F32),
            pltpu.VMEM((NLEV, 8, 128), F32),
            pltpu.VMEM((NLEV, NLEV, 8, 128), F32),
            pltpu.VMEM((NLEV, 8, 128), F32),
            pltpu.VMEM((NTILE, 8, 128), F32),
            pltpu.VMEM((TR, 2 * LAT, LOOK), BF16),
            pltpu.VMEM((PER, 2 * TR * LAT), F32),
            dma((10,)),
            dma((8,)), dma((8,)),
            dma((2,)), dma((2,)),
            dma((3, 2)), dma((3, 2)),
            dma((NTILE,)), dma((NTILE,)),
            dma((NLEV, NLEV)), dma((NLEV, NLEV)),
            dma((NTILE,)), dma((NTILE,)),
        ],
        compiler_params=pltpu.CompilerParams(
            collective_id=0, has_side_effects=True, vmem_limit_bytes=60 * 1024 * 1024
        ),
    )(
        conc, u_wind, v_wind, mixing, kernels, observed, obs_weight[None], column_tile.T, footprint.T, kernel_index[None]
    )
    return pl.pallas_call(
        store,
        out_shape=shapes,
        in_specs=[hbm] * 2,
        out_specs=(hbm, hbm),
        scratch_shapes=[
            pltpu.VMEM((TR, SND), F32),
            pltpu.VMEM((TR, LV, LON, LAT), F32),
            dma((TR + 1,)),
            dma((TR + 1,)),
        ],
        compiler_params=pltpu.CompilerParams(vmem_limit_bytes=60 * 1024 * 1024),
    )(*found)


def solution(mesh):
    placed = (
        P(None, "lev", "tile", None),
        P("lev", "tile", None),
        P("lev", "tile", None),
        P("lev", "tile", None),
        P(None, "lev"),
        P(None, "tile"),
        P("tile"),
        P("tile", None),
        P("tile", None),
        P("tile"),
    )
    return jax.shard_map(
        body,
        mesh=mesh,
        in_specs=placed,
        out_specs=(P(None, "tile"), P(None, "lev", "tile", None)),
        check_vma=False,
    )
```
